128 devices in a mesh: image: 8 (over x_hi, y), patch: 16 (over x_lo, z, core).
Axes of the slice: x: 4 (x_hi: 2, x_lo: 2; x = x_hi * 2 + x_lo), y: 4, z: 4, core: 2. Of those that a mesh axis runs over, the one named last changes fastest.
Arguments:
- images: bfloat16 [8, 128, 64, 640], P('image', 'patch'), may hold values from -8 to 8
- heights: int32 [8], P('image'), may hold values from 8 to 128, as said below
- opening_scale_vector: float32 [640], replicated, may hold values from 0.25 to 1.75
- opening_offset_vector: float32 [640], replicated, may hold values from -3 to 3
- conv_weight: bfloat16 [3, 3, 640, 640], P(None, None, 'image'), may hold values from -0.078125 to 0.078125
- kernel_offset_vector: float32 [640], replicated, may hold values from -3 to 3
- closing_scale_vector: float32 [640], replicated, may hold values from 0.25 to 1.75
- closing_offset_vector: float32 [640], replicated, may hold values from -3 to 3
- query_weight: bfloat16 [640, 640], replicated, may hold values from -1 to 1
- key_weight: bfloat16 [640, 640], replicated, may hold values from -1 to 1
- value_weight: bfloat16 [640, 640], replicated, may hold values from -0.25 to 0.25
- out_weight: bfloat16 [640, 640], replicated, may hold values from -0.25 to 0.25
- out_bias: float32 [640], replicated, may hold values from -3 to 3
Outputs:
- block_features: bfloat16 [8, 128, 64, 640], P('image', 'patch')
The draws below stay inside these ranges and needn't reach their ends.
Inputs may be any that keep to these rules, and one draw needn't show every extreme that they name: `heights`: every image uses at least 8 rows; in every batch some image uses all 128 rows.
All inputs are finite; a program needn't handle non-finite values.
Results may differ from the reference program's by a relative error of at most 0.0124.
The reference program's roundings to bfloat16 on the way count: a program that leaves them out, or rounds other values in their place, can miss the bound.
Values may be sent and summed in bfloat16 or wider, within the bound.
No kernel may reach another device: no remote copies, remote signals or barrier semaphores. Data moves between devices by JAX's collectives and lax.ppermute only.
A program may use at most 384 MiB of HBM per device.

```python
import math
import jax
import jax.numpy as jnp
from jax import lax

C = 640
HEAD_DIM = 64
GROUPS = 32
RP = 8
W = 64
H_MAX = 128
IMAGES = 8


def draw_images(key, part):
    key = jax.random.fold_in(key, 11)
    core_key, scale_key, group_key, channel_key, phase_key = jax.random.split(key, 5)
    position = jnp.arange(H_MAX, dtype=jnp.float32)[None, :, None, None] / H_MAX
    row_phase = jax.random.uniform(phase_key, (IMAGES, 1, 1, 1), jnp.float32, -3.14159, 3.14159)
    row_trend = 1.2 * (2.0 * position - 1.0) + 0.8 * jnp.sin(12.566371 * position + row_phase)
    group_level = jnp.repeat(jax.random.normal(group_key, (1, 1, 1, GROUPS), jnp.float32), C // GROUPS, axis=3)
    direction = group_level + 0.4 * jax.random.normal(channel_key, (1, 1, 1, C), jnp.float32)
    row_scale = jnp.exp(jax.random.uniform(scale_key, (IMAGES, H_MAX, 1, 1), jnp.float32, -1.2, 1.1))
    core = jax.random.normal(core_key, (IMAGES, H_MAX, W, C), jnp.float32)
    values = core * row_scale + row_trend * direction
    return jnp.clip(values, -8.0, 8.0).astype(jnp.bfloat16)


def draw_heights(key, part):
    key = jax.random.fold_in(key, 12)
    opening_result, closing_result = jax.random.split(key)
    values = jax.random.randint(opening_result, (IMAGES,), RP, H_MAX + 1)
    chosen = jax.random.randint(closing_result, (), 0, IMAGES)
    return jnp.where(jnp.arange(IMAGES) == chosen, H_MAX, values).astype(jnp.int32)


def draw_query_weight(key, part):
    key = jax.random.fold_in(key, 13)
    own = jax.random.normal(key, (C, C), jnp.float32) * C ** (-0.5)
    values = own
    return jnp.clip(values, -1.0, 1.0).astype(jnp.bfloat16)


def draw_key_weight(key, part):
    key = jax.random.fold_in(key, 14)
    own = jax.random.normal(key, (C, C), jnp.float32) * C ** (-0.5)
    values = own
    return jnp.clip(values, -1.0, 1.0).astype(jnp.bfloat16)


def block_scale(key, shape, pieces, low, high):
    def one(dim, blocks):
        steps = jax.random.uniform(jax.random.fold_in(jax.random.fold_in(key, 6), dim), (blocks,), jnp.float32, low / len(pieces), high / len(pieces))
        return jnp.repeat(jnp.exp(steps), shape[dim] // blocks).reshape((-1,) + (1,) * (len(shape) - dim - 1))

    factor_of = one(*pieces[0])
    for cut in pieces[1:]:
        factor_of = factor_of * one(*cut)
    return factor_of


def gaussian(key, extent, width, limit, pieces=(), kind=jnp.bfloat16):
    drawn = jax.random.normal(key, extent, jnp.float32) * width
    if len(pieces) > 0:
        drawn = block_scale(key, extent, pieces, -0.22, 0.18) * drawn
    return jnp.clip(drawn, min=-limit, max=limit).astype(kind)


def setup_inputs(seed: int = 0) -> dict:
    splits = jax.random.split(jax.random.key(seed), 14)
    images = draw_images(jax.random.fold_in(splits[13], 71), 0)
    heights = draw_heights(jax.random.fold_in(splits[13], 71), 0)
    opening_scale_vector = jnp.clip(1.0 + 0.15 * jax.random.normal(splits[2], (C,), jnp.float32), 0.25, 1.75)
    opening_offset_vector = gaussian(splits[3], (C,), 0.5, 3.0, (), jnp.float32)
    conv_weight = gaussian(splits[4], (3, 3, C, C), (9 * C) ** -0.5, 0.078125, ((2, 8),))
    kernel_offset_vector = gaussian(splits[5], (C,), 0.5, 3.0, (), jnp.float32)
    closing_scale_vector = jnp.clip(1.0 + 0.15 * jax.random.normal(splits[6], (C,), jnp.float32), 0.25, 1.75)
    closing_offset_vector = gaussian(splits[7], (C,), 0.5, 3.0, (), jnp.float32)
    query_weight = draw_query_weight(jax.random.fold_in(splits[13], 71), 0)
    key_weight = draw_key_weight(jax.random.fold_in(splits[13], 71), 0)
    value_weight = gaussian(splits[10], (C, C), C ** -0.5, 0.25)
    out_weight = gaussian(splits[11], (C, C), C ** -0.5, 0.25)
    out_bias = gaussian(splits[12], (C,), 0.5, 3.0, (), jnp.float32)
    return dict(images=images, heights=heights, opening_scale_vector=opening_scale_vector, opening_offset_vector=opening_offset_vector, conv_weight=conv_weight, kernel_offset_vector=kernel_offset_vector, closing_scale_vector=closing_scale_vector, closing_offset_vector=closing_offset_vector, query_weight=query_weight, key_weight=key_weight, value_weight=value_weight, out_weight=out_weight, out_bias=out_bias)


def cluster_standardizer(values, occupied_flags, gain, shift, entries_number):
    pixel_down, pixel_across, feature_depth = values.shape
    grouped = values.reshape(pixel_down, pixel_across, GROUPS, feature_depth // GROUPS)
    weight = occupied_flags.astype(jnp.float32)[:, None, None, None]
    mean = lax.optimization_barrier(jnp.sum(grouped * weight, axis=(0, 1, 3))) / entries_number
    centred = (grouped - mean[None, None, :, None]) * weight
    spread = lax.optimization_barrier(jnp.sum(centred * centred, axis=(0, 1, 3))) / entries_number
    scaled = (grouped - mean[None, None, :, None]) * lax.rsqrt(spread + 1e-05)[None, None, :, None]
    return scaled.reshape(pixel_down, pixel_across, feature_depth) * gain + shift

def convolve(kernel_neighbourhood, weight):
    pixel_down, pixel_across, feature_depth = kernel_neighbourhood.shape
    padded = jnp.pad(kernel_neighbourhood, ((1, 1), (1, 1), (0, 0)))
    cumulative_summed = jnp.zeros((pixel_down * pixel_across, weight.shape[3]), jnp.float32)
    for step_y in range(3):
        for step_x in range(3):
            window = padded[step_y:step_y + pixel_down, step_x:step_x + pixel_across].reshape(pixel_down * pixel_across, feature_depth)
            cumulative_summed = cumulative_summed + jnp.dot(window, weight[step_y, step_x], preferred_element_type=jnp.float32)
    return cumulative_summed

def attend_image(query, keys, values, height, pixel_across):
    tokens, feature_depth = query.shape
    heads = feature_depth // HEAD_DIM
    block = math.gcd(tokens, 512)
    key_heads = keys.astype(jnp.float32).reshape(tokens, heads, HEAD_DIM)
    value_heads = values.astype(jnp.float32).reshape(tokens, heads, HEAD_DIM)
    live_keys = jnp.arange(tokens, dtype=jnp.int32) // pixel_across < height

    def one_block(rows_q):
        query_heads = rows_q.astype(jnp.float32).reshape(block, heads, HEAD_DIM)
        scores = jnp.einsum('qhd,khd->hqk', query_heads, key_heads) * HEAD_DIM ** (-0.5)
        scores = jnp.where(live_keys[None, None, :], scores, -1e+30)
        top = lax.optimization_barrier(jnp.max(scores, axis=-1, keepdims=True))
        weights = jnp.exp(scores - top)
        cumulative_summed = lax.optimization_barrier(jnp.sum(weights, axis=-1))
        rounded = weights.astype(jnp.bfloat16).astype(jnp.float32)
        mixed = jnp.einsum('hqk,khd->qhd', rounded, value_heads)
        return (mixed / jnp.transpose(cumulative_summed)[:, :, None]).reshape(block, feature_depth).astype(jnp.bfloat16)
    blocks = lax.map(one_block, query.reshape(tokens // block, block, feature_depth))
    return blocks.reshape(tokens, feature_depth)

def one_image(kernel_neighbourhood, height, opening_scale_vector, opening_offset_vector, conv_weight, kernel_offset_vector, closing_scale_vector, closing_offset_vector, query_weight, key_weight, value_weight, out_weight, out_bias):
    pixel_down, pixel_across, feature_depth = kernel_neighbourhood.shape
    occupied_flags = jnp.arange(pixel_down, dtype=jnp.int32) < height
    line_occupancy = occupied_flags.astype(jnp.float32)[:, None, None]
    entries_number = (height * pixel_across * (feature_depth // GROUPS)).astype(jnp.float32)
    opening_position = kernel_neighbourhood.astype(jnp.float32) * line_occupancy
    opening_result = (jax.nn.silu(cluster_standardizer(opening_position, occupied_flags, opening_scale_vector, opening_offset_vector, entries_number)) * line_occupancy).astype(jnp.bfloat16)
    spatial_filter_picture = convolve(opening_result, conv_weight).reshape(pixel_down, pixel_across, feature_depth)
    skip_source = ((opening_position + spatial_filter_picture + kernel_offset_vector) * line_occupancy).astype(jnp.bfloat16)
    closing_result = (cluster_standardizer(skip_source.astype(jnp.float32), occupied_flags, closing_scale_vector, closing_offset_vector, entries_number) * line_occupancy).astype(jnp.bfloat16)
    flat = closing_result.reshape(pixel_down * pixel_across, feature_depth)
    query = jnp.dot(flat, query_weight, preferred_element_type=jnp.float32).astype(jnp.bfloat16)
    keys = jnp.dot(flat, key_weight, preferred_element_type=jnp.float32).astype(jnp.bfloat16)
    values = jnp.dot(flat, value_weight, preferred_element_type=jnp.float32).astype(jnp.bfloat16)
    mixed = attend_image(query, keys, values, height, pixel_across)
    cumulative_summed = skip_source.astype(jnp.float32).reshape(pixel_down * pixel_across, feature_depth)
    cumulative_summed = cumulative_summed + jnp.dot(mixed, out_weight, preferred_element_type=jnp.float32) + out_bias
    return (cumulative_summed.reshape(pixel_down, pixel_across, feature_depth) * line_occupancy).astype(jnp.bfloat16)

def reference(images, heights, opening_scale_vector, opening_offset_vector, conv_weight, kernel_offset_vector, closing_scale_vector, closing_offset_vector, query_weight, key_weight, value_weight, out_weight, out_bias):

    def apply(pair):
        kernel_neighbourhood, height = pair
        return one_image(kernel_neighbourhood, height, opening_scale_vector, opening_offset_vector, conv_weight, kernel_offset_vector, closing_scale_vector, closing_offset_vector, query_weight, key_weight, value_weight, out_weight, out_bias)
    return lax.map(apply, (images, heights))
```

```python
import functools

import jax
import jax.numpy as jnp
from jax import lax
from jax.experimental import pallas as pl
from jax.experimental.pallas import tpu as pltpu
from jax.sharding import PartitionSpec as P

HEAD_DIM = 64
GROUPS = 32
C = 640
W = 64
RP = 8
TOK = RP * W
HEADS = C // HEAD_DIM
PAIRS = HEADS // 2
VROWS = 80
HALF = 368
BOTH = ("image", "patch")
SCORE_SCALE = HEAD_DIM**-0.5 * 1.4426950408889634
VMEM = pl.BlockSpec(memory_space=pltpu.VMEM)
SMEM = pl.BlockSpec(memory_space=pltpu.SMEM)
ANY = pl.BlockSpec(memory_space=pl.ANY)
F32 = jnp.float32
BF16 = jnp.bfloat16


def params(mib):
    return pltpu.CompilerParams(vmem_limit_bytes=mib << 20)


def shape(dims, kind):
    return jax.ShapeDtypeStruct(dims, kind)


def pairs_of(move):
    pairs = []
    for x in range(4):
        for y in range(4):
            for z in range(4):
                for core in range(2):
                    ends = []
                    for a, b, c, d in ((x, y, z, core), move(x, y, z, core)):
                        a, b, c = a % 4, b % 4, c % 4
                        ends.append((a // 2 * 4 + b) * 16 + a % 2 * 8 + c * 2 + d)
                    pairs.append(tuple(ends))
    return pairs


SIBLING = pairs_of(lambda x, y, z, core: (x, y, z, 1 - core))
Y_UP = pairs_of(lambda x, y, z, core: (x, y + 1, z, core))
Y_DOWN = pairs_of(lambda x, y, z, core: (x, y - 1, z, core))
Z_UP = pairs_of(lambda x, y, z, core: (x, y, z + 1, core))
Z_DOWN = pairs_of(lambda x, y, z, core: (x, y, z - 1, core))
X_LO = pairs_of(lambda x, y, z, core: (x ^ 1, y, z, core))
X_HI = pairs_of(lambda x, y, z, core: (3 - x, y, z, core))


def send(block, pairs):
    return lax.ppermute(block, BOTH, pairs)


def row_live(count, first_row, height):
    rows = lax.broadcasted_iota(jnp.int32, (count, 1), 0) // W + first_row
    return jnp.where(jnp.logical_and(rows >= 0, rows < height), 1.0, 0.0)


def channel_stats(cells, live, live_count, out_ref):
    mean = jnp.sum(cells * live, axis=0, keepdims=True) / jnp.maximum(live_count, 1.0)
    centred = (cells - mean) * live
    out_ref[0:1, :] = mean
    out_ref[1:2, :] = jnp.sum(centred * centred, axis=0, keepdims=True)


def stats_kernel(place_ref, image_ref, out_ref):
    first_row, height = place_ref[0], place_ref[1]
    count = (jnp.clip(height - first_row, 0, RP) * W).astype(F32)
    channel_stats(image_ref[...].astype(F32), row_live(TOK, first_row, height), count, out_ref)


def activate_kernel(place_ref, image_ref, above_ref, below_ref, affine_ref, out_ref):
    first_row, height = place_ref[0], place_ref[1]
    mean, gain, shift = affine_ref[0:1, :], affine_ref[1:2, :], affine_ref[2:3, :]

    def put(at, count, block, row):
        live = row_live(count, row, height)
        v = (block.astype(F32) * live - mean) * gain + shift
        out_ref[at : at + count, :] = (v / (1.0 + jnp.exp(-v)) * live).astype(BF16)

    put(0, W, above_ref[...], first_row - 1)
    put(W, TOK, image_ref[...], first_row)
    put(W + TOK, W, below_ref[...], first_row + RP)


def conv_kernel(place_ref, first_ref, image_ref, bias_ref, own_ref, *refs):
    mine, theirs = refs[:7], refs[7:14]
    resid_ref, stats_ref, kernel, sem = refs[14:]
    first_row, height, core = place_ref[0], place_ref[1], place_ref[2]
    order = [dy * 3 + dx for dx in range(3) for dy in range(3)]

    def load(source, rows, count, tap, channel):
        pltpu.make_async_copy(
            source.at[pl.ds(rows, count), :],
            kernel.at[tap, pl.ds(pl.multiple_of(channel, 16), count), :],
            sem.at[tap],
        ).start()

    def load_all(lows, highs):
        for tap in order:
            for i in range(7):
                channel = place_ref[4 + i] * 80
                if tap <= 3:
                    load(lows[i], 80 * tap, 80, tap, channel)
                elif tap >= 5:
                    load(highs[i], 80 * tap - 352, 80, tap, channel)
                else:
                    load(lows[i], 320, 48, tap, channel)
                    load(highs[i], 16, 32, tap, channel + 48)

    for tap in order:
        load(own_ref, 80 * tap, 80, tap, place_ref[3] * 80)
    pl.when(core == 0)(lambda: load_all(mine, theirs))
    pl.when(core != 0)(lambda: load_all(theirs, mine))

    columns = lax.broadcasted_iota(jnp.int32, (TOK, 1), 0) % W
    total = None
    for dx in (0, 1, 2):
        part = None
        for dy in range(3):
            tap = dy * 3 + dx
            pltpu.make_async_copy(kernel.at[tap], kernel.at[tap], sem.at[tap]).wait()
            product = jnp.dot(
                first_ref[dy * W : dy * W + TOK, :], kernel[tap], preferred_element_type=F32
            )
            part = product if part is None else part + product
        if dx == 0:
            part = jnp.where(columns == 0, 0.0, pltpu.roll(part, 1, 0))
        if dx == 2:
            part = jnp.where(columns == W - 1, 0.0, pltpu.roll(part, TOK - 1, 0))
        total = part if total is None else total + part
    live = row_live(TOK, first_row, height)
    start = image_ref[...].astype(F32) * live
    resid = ((start + total + bias_ref[...]) * live).astype(BF16)
    resid_ref[...] = resid
    count = (jnp.clip(height - first_row, 0, RP) * W).astype(F32)
    channel_stats(resid.astype(F32), live, count, stats_ref)


def second_kernel(place_ref, resid_ref, affine_ref, out_ref):
    mean, gain, shift = affine_ref[0:1, :], affine_ref[1:2, :], affine_ref[2:3, :]
    live = row_live(TOK, place_ref[0], place_ref[1])
    v = (resid_ref[...].astype(F32) - mean) * gain + shift
    out_ref[...] = (v * live).astype(BF16)


def transposed(weight_t, block):
    return lax.dot_general(
        weight_t, block, (((1,), (1,)), ((), ())), preferred_element_type=F32
    ).astype(BF16)


def put_values(place_ref, at, weight_ref, block, n, values_ref):
    tokens = lax.broadcasted_iota(jnp.int32, (VROWS - HEAD_DIM, TOK), 1)
    lines = lax.broadcasted_iota(jnp.int32, (VROWS - HEAD_DIM, TOK), 0)
    rows = tokens // W + place_ref[at]
    ones = jnp.where(jnp.logical_and(lines == 0, rows < place_ref[1]), 1.0, 0.0).astype(BF16)
    values = transposed(weight_ref[...], block)
    span = slice(n * TOK, (n + 1) * TOK)
    for h in range(HEADS):
        values_ref[h, 0:HEAD_DIM, span] = values[h * HEAD_DIM : (h + 1) * HEAD_DIM]
        values_ref[h, HEAD_DIM:VROWS, span] = ones


def query_kernel(second_ref, wq_ref, out_ref):
    q = transposed(wq_ref[...], second_ref[...])
    zero = jnp.zeros((HEAD_DIM, TOK), BF16)
    for p in range(PAIRS):
        a = p * 2 * HEAD_DIM
        out_ref[p, 0:HEAD_DIM, 0:TOK] = q[a : a + HEAD_DIM]
        out_ref[p, 0:HEAD_DIM, TOK : 2 * TOK] = zero
        out_ref[p, HEAD_DIM : 2 * HEAD_DIM, 0:TOK] = zero
        out_ref[p, HEAD_DIM : 2 * HEAD_DIM, TOK : 2 * TOK] = q[a + HEAD_DIM : a + 2 * HEAD_DIM]


def project_kernel(sizes, place_ref, *refs):
    blocks = refs[: len(sizes)]
    wk_ref, wv_ref, keys_ref, values_ref, held = refs[len(sizes) :]
    at = 0
    for ref, size in zip(blocks, sizes):
        held[at : at + size, :] = ref[...]
        at += size
    for n in range(at // TOK):
        block = held[n * TOK : (n + 1) * TOK, :]
        keys_ref[n * TOK : (n + 1) * TOK, :] = jnp.dot(
            block, wk_ref[...], preferred_element_type=F32
        ).astype(BF16)
        put_values(place_ref, 2 + n, wv_ref, block, n, values_ref)


def open_kernel(query_ref, keys_ref, values_ref, acc_ref, top_ref):
    for p in range(PAIRS):
        span = slice(p * 2 * HEAD_DIM, (p + 1) * 2 * HEAD_DIM)
        s = jnp.dot(keys_ref[:, span], query_ref[p], preferred_element_type=F32) * SCORE_SCALE
        top = jnp.max(s, axis=0, keepdims=True)
        top_ref[p] = jnp.broadcast_to(top, (8, 2 * TOK))
        weights = jnp.exp2(s - top).astype(BF16)
        for h in range(2):
            acc_ref[2 * p + h] = jnp.dot(
                values_ref[2 * p + h],
                weights[:, h * TOK : (h + 1) * TOK],
                preferred_element_type=F32,
            )


def attend_kernel(query_ref, top_ref, keys_ref, values_ref, held_ref, acc_ref):
    @pl.when(pl.program_id(0) == 0)
    def _():
        acc_ref[...] = held_ref[...]

    for p in range(PAIRS):
        span = slice(p * 2 * HEAD_DIM, (p + 1) * 2 * HEAD_DIM)
        s = jnp.dot(keys_ref[:, span], query_ref[p], preferred_element_type=F32)
        weights = jnp.exp2(s * SCORE_SCALE - top_ref[p, 0:1, :]).astype(BF16)
        for h in range(2):
            acc_ref[2 * p + h] += jnp.dot(
                values_ref[2 * p + h],
                weights[:, h * TOK : (h + 1) * TOK],
                preferred_element_type=F32,
            )


def finish_kernel(place_ref, acc_ref, resid_ref, wo_ref, bias_ref, out_ref, far_ref):
    mixed = []
    far = jnp.zeros((1, TOK), F32)
    for h in range(HEADS):
        total = acc_ref[h, HEAD_DIM : HEAD_DIM + 1, :]
        inside = jnp.logical_and(total > 2.0**-60, total < 2.0**100)
        far = jnp.maximum(far, jnp.where(inside, 0.0, 1.0))
        mixed.append((acc_ref[h, 0:HEAD_DIM, :] / total).astype(BF16))
    far_ref[0, 0] = jnp.max(far).astype(jnp.int32)
    update = lax.dot_general(
        jnp.concatenate(mixed, axis=0),
        wo_ref[...],
        (((0,), (0,)), ((), ())),
        preferred_element_type=F32,
    )
    live = row_live(TOK, place_ref[0], place_ref[1])
    out_ref[...] = ((resid_ref[...].astype(F32) + update + bias_ref[...]) * live).astype(BF16)


def exact_attention(query, keys, values, resid, out_weight, out_bias, live):
    keys = jnp.concatenate(keys, axis=0)
    values = jnp.concatenate(values, axis=2)
    key_live = values[0, HEAD_DIM] > 0

    def one_head(h):
        q = lax.dynamic_slice(
            query, (h // 2, h % 2 * HEAD_DIM, h % 2 * TOK), (1, HEAD_DIM, TOK)
        )[0]
        k = lax.dynamic_slice(keys, (0, h * HEAD_DIM), (keys.shape[0], HEAD_DIM))
        v = lax.dynamic_slice(values, (h, 0, 0), (1, HEAD_DIM, keys.shape[0]))[0]
        s = jnp.dot(k, q, preferred_element_type=F32) * HEAD_DIM**-0.5
        s = jnp.where(key_live[:, None], s, -1e30)
        weights = jnp.exp(s - jnp.max(s, axis=0, keepdims=True))
        total = jnp.sum(weights, axis=0, keepdims=True)
        return (jnp.dot(v, weights.astype(BF16), preferred_element_type=F32) / total).astype(BF16)

    mixed = lax.map(one_head, jnp.arange(HEADS, dtype=jnp.int32)).reshape(C, TOK)
    update = lax.dot_general(
        mixed, out_weight, (((0,), (0,)), ((), ())), preferred_element_type=F32
    )
    return ((resid.astype(F32) + update + out_bias[None, :]) * live).astype(BF16)


def combine(stats, height, gain, shift):
    everyone = lax.all_to_all(
        jnp.broadcast_to(stats[None], (16,) + stats.shape), "patch", 0, 0, tiled=False
    )
    rows = jnp.clip(height - RP * jnp.arange(16, dtype=jnp.int32), 0, RP)
    counts = (rows * W).astype(F32)[:, None, None]
    entries = (height * W * (C // GROUPS)).astype(F32)
    means = everyone[:, 0].reshape(16, GROUPS, C // GROUPS)
    squares = everyone[:, 1].reshape(16, GROUPS, C // GROUPS)
    mean = jnp.sum(means * counts, axis=(0, 2)) / entries
    apart = means - mean[None, :, None]
    spread = jnp.sum(squares + counts * apart * apart, axis=(0, 2)) / entries
    scale = lax.rsqrt(spread + 1e-05)
    wide = lambda v: jnp.broadcast_to(v[:, None], (GROUPS, C // GROUPS)).reshape(C)
    return jnp.stack([wide(mean), wide(scale) * gain, shift])


def per_device(
    images,
    heights,
    opening_scale_vector,
    opening_offset_vector,
    conv_weight,
    kernel_offset_vector,
    closing_scale_vector,
    closing_offset_vector,
    query_weight,
    key_weight,
    value_weight,
    out_weight,
    out_bias,
):
    image = images[0].reshape(TOK, C)
    height = heights[0]
    at_image = lax.axis_index("image")
    at_patch = lax.axis_index("patch")
    core = at_patch % 2
    first_row = at_patch * RP
    place = jnp.stack([first_row, height])

    own = conv_weight.reshape(9 * 80, C)
    half = lax.dynamic_slice(own, (core * (720 - HALF), 0), (HALF, C))
    a_up = send(half, Y_UP)
    a_down = send(half, Y_DOWN)
    b_own = send(half, X_HI)
    up_pairs = [(g * 16 + i, g * 16 + i + 1) for g in range(8) for i in range(15)]
    above = send(image[TOK - W :], up_pairs)
    below = send(image[:W], [(b, a) for a, b in up_pairs])

    stats = pl.pallas_call(
        stats_kernel,
        in_specs=[SMEM, VMEM],
        out_specs=VMEM,
        out_shape=shape((2, C), F32),
        compiler_params=params(16),
    )(place, image)
    affine = combine(stats, height, opening_scale_vector, opening_offset_vector)

    a_far = send(a_up, Y_UP)
    b_up = send(a_up, X_HI)
    b_down = send(b_own, Y_DOWN)
    first = pl.pallas_call(
        activate_kernel,
        in_specs=[SMEM] + [VMEM] * 4,
        out_specs=VMEM,
        out_shape=shape((TOK + 2 * W, C), BF16),
        compiler_params=params(16),
    )(place, image, above, below, affine)

    b_far = jnp.concatenate(
        [
            send(a_far[:128], X_HI),
            send(b_up[128:256], Y_UP),
            send(b_down[256:], Y_DOWN),
        ],
        axis=0,
    )
    mine = [a_up, a_down, b_own, a_far, b_up, b_down, b_far]
    theirs = [send(block, SIBLING) for block in mine]
    x_hi, y = at_image // 4, at_image % 4
    a_at = lambda by: x_hi * 4 + (y + by) % 4
    b_at = lambda by: (1 - x_hi) * 4 + (y + by) % 4
    conv_place = jnp.stack(
        [first_row, height, core, at_image]
        + [a_at(3), a_at(1), b_at(0), a_at(2), b_at(3), b_at(1), b_at(2)]
    )
    resid, stats = pl.pallas_call(
        conv_kernel,
        in_specs=[SMEM, VMEM, VMEM, VMEM] + [ANY] * 15,
        out_specs=[VMEM, VMEM],
        out_shape=[shape((TOK, C), BF16), shape((2, C), F32)],
        scratch_shapes=[pltpu.VMEM((9, C, C), BF16), pltpu.SemaphoreType.DMA((9,))],
        compiler_params=params(40),
    )(conv_place, first, image, kernel_offset_vector[None, :], own, *mine, *theirs)
    affine = combine(stats, height, closing_scale_vector, closing_offset_vector)
    second = pl.pallas_call(
        second_kernel,
        in_specs=[SMEM, VMEM, VMEM],
        out_specs=VMEM,
        out_shape=shape((TOK, C), BF16),
        compiler_params=params(16),
    )(place, resid, affine)

    x_lo, z = at_patch // 8, at_patch // 2 % 4
    c_row = lambda by: (x_lo * 8 + (z + by) % 4 * 2 + core) * RP
    d_row = lambda by: ((1 - x_lo) * 8 + (z + by) % 4 * 2 + core) * RP
    wv_t, wq_t = value_weight.T, query_weight.T

    def project(blocks, rows):
        sizes = [block.shape[0] for block in blocks]
        count = sum(sizes)
        return pl.pallas_call(
            functools.partial(project_kernel, sizes),
            in_specs=[SMEM] + [VMEM] * (len(blocks) + 2),
            out_specs=[VMEM, VMEM],
            out_shape=[shape((count, C), BF16), shape((HEADS, VROWS, count), BF16)],
            scratch_shapes=[pltpu.VMEM((count, C), BF16)],
            compiler_params=params(32),
        )(jnp.stack([first_row, height] + rows), *blocks, key_weight, wv_t)

    def swap(pair):
        return [send(pair[0], SIBLING), send(pair[1], SIBLING)]

    acc_shape = (HEADS, VROWS, TOK)

    def attend(pair, acc):
        count = pair[0].shape[0]
        return pl.pallas_call(
            attend_kernel,
            grid=(count // TOK,),
            in_specs=[
                pl.BlockSpec((PAIRS, 2 * HEAD_DIM, 2 * TOK), lambda i: (0, 0, 0)),
                pl.BlockSpec((PAIRS, 8, 2 * TOK), lambda i: (0, 0, 0)),
                pl.BlockSpec((TOK, C), lambda i: (i, 0)),
                pl.BlockSpec((HEADS, VROWS, TOK), lambda i: (0, 0, i)),
                pl.BlockSpec(acc_shape, lambda i: (0, 0, 0)),
            ],
            out_specs=pl.BlockSpec(acc_shape, lambda i: (0, 0, 0)),
            out_shape=shape(acc_shape, F32),
            input_output_aliases={4: 0},
            compiler_params=params(40),
            cost_estimate=pl.CostEstimate(
                flops=count * TOK * C * 16, bytes_accessed=count * C * 4, transcendentals=0
            ),
        )(query, top, pair[0], pair[1], acc)

    c_up = send(second, Z_UP)
    c_down = send(second, Z_DOWN)
    d_own = send(second, X_LO)
    stage_0 = project([second], [c_row(0)])
    other_0 = swap(stage_0)
    query = pl.pallas_call(
        query_kernel,
        in_specs=[VMEM, VMEM],
        out_specs=VMEM,
        out_shape=shape((PAIRS, 2 * HEAD_DIM, 2 * TOK), BF16),
        compiler_params=params(16),
    )(second, wq_t)
    acc, top = pl.pallas_call(
        open_kernel,
        in_specs=[VMEM] * 3,
        out_specs=[VMEM] * 2,
        out_shape=[shape(acc_shape, F32), shape((PAIRS, 8, 2 * TOK), F32)],
        compiler_params=params(40),
        cost_estimate=pl.CostEstimate(
            flops=TOK * TOK * C * 16, bytes_accessed=TOK * C * 4, transcendentals=0
        ),
    )(query, *stage_0)
    acc = attend(other_0, acc)

    c_far = send(c_up, Z_UP)
    d_up = send(c_up, X_LO)
    d_down = send(d_own, Z_DOWN)
    stage_1 = project([c_up, c_down, d_own], [c_row(3), c_row(1), d_row(0)])
    other_1 = swap(stage_1)
    acc = attend(stage_1, acc)
    acc = attend(other_1, acc)

    d_far = [send(c_far[:176], X_LO), send(d_up[176:352], Z_UP), send(d_down[352:], Z_DOWN)]
    stage_2 = project([c_far, d_up, d_down], [c_row(2), d_row(3), d_row(1)])
    other_2 = swap(stage_2)
    acc = attend(stage_2, acc)
    acc = attend(other_2, acc)

    stage_3 = project(d_far, [d_row(2)])
    other_3 = swap(stage_3)
    acc = attend(stage_3, acc)
    acc = attend(other_3, acc)

    out, far = pl.pallas_call(
        finish_kernel,
        in_specs=[SMEM] + [VMEM] * 4,
        out_specs=[VMEM, SMEM],
        out_shape=[shape((TOK, C), BF16), shape((1, 1), jnp.int32)],
        compiler_params=params(32),
    )(place, acc, resid, out_weight, out_bias[None, :])
    stages = [stage_0, other_0, stage_1, other_1, stage_2, other_2, stage_3, other_3]
    live = ((jnp.arange(TOK, dtype=jnp.int32) // W + first_row) < height).astype(F32)[:, None]
    out = lax.cond(
        far[0, 0] > 0,
        lambda: exact_attention(
            query,
            [s[0] for s in stages],
            [s[1] for s in stages],
            resid,
            out_weight,
            out_bias,
            live,
        ),
        lambda: out,
    )
    return out.reshape(1, RP, W, C)


def solution(mesh):
    in_specs = (
        P("image", "patch", None, None),
        P("image"),
        P(),
        P(),
        P(None, None, "image", None),
        P(),
        P(),
        P(),
        P(),
        P(),
        P(),
        P(),
        P(),
    )
    out_specs = P("image", "patch", None, None)
    return jax.shard_map(
        per_device, mesh=mesh, in_specs=in_specs, out_specs=out_specs, check_vma=False
    )
```

```python
import functools

import jax
import jax.numpy as jnp
from jax import lax
from jax.experimental import pallas as pl
from jax.experimental.pallas import tpu as pltpu
from jax.sharding import PartitionSpec as P

HEAD_DIM = 64
GROUPS = 32
C = 640
W = 64
RP = 8
TOK = RP * W
HEADS = C // HEAD_DIM
VROWS = 80
MINE = HEADS // 2
HALF_C = C // 2
QUERIES = 2 * TOK
HALF = 368
BOTH = ("image", "patch")
SCORE_SCALE = HEAD_DIM**-0.5 * 1.4426950408889634
VMEM = pl.BlockSpec(memory_space=pltpu.VMEM)
SMEM = pl.BlockSpec(memory_space=pltpu.SMEM)
ANY = pl.BlockSpec(memory_space=pl.ANY)
HBM = pl.BlockSpec(memory_space=pltpu.HBM)
F32 = jnp.float32
BF16 = jnp.bfloat16


def params(mib):
    return pltpu.CompilerParams(vmem_limit_bytes=mib << 20)


def cost(microseconds):
    return pl.CostEstimate(
        flops=int(microseconds * 1e9), bytes_accessed=int(microseconds * 3e6), transcendentals=0
    )


def near(dims, kind):
    return pltpu.VMEM(dims, kind)


def shape(dims, kind):
    return jax.ShapeDtypeStruct(dims, kind)


def pairs_of(move):
    pairs = []
    for x in range(4):
        for y in range(4):
            for z in range(4):
                for core in range(2):
                    ends = []
                    for a, b, c, d in ((x, y, z, core), move(x, y, z, core)):
                        a, b, c = a % 4, b % 4, c % 4
                        ends.append((a // 2 * 4 + b) * 16 + a % 2 * 8 + c * 2 + d)
                    pairs.append(tuple(ends))
    return pairs


SIBLING = pairs_of(lambda x, y, z, core: (x, y, z, 1 - core))
SIBLINGS = [SIBLING, SIBLING[1:] + SIBLING[:1], SIBLING[2:] + SIBLING[:2]]
Y_UP = pairs_of(lambda x, y, z, core: (x, y + 1, z, core))
Y_DOWN = pairs_of(lambda x, y, z, core: (x, y - 1, z, core))
Z_UP = pairs_of(lambda x, y, z, core: (x, y, z + 1, core))
Z_DOWN = pairs_of(lambda x, y, z, core: (x, y, z - 1, core))
X_LO = pairs_of(lambda x, y, z, core: (x ^ 1, y, z, core))
X_HI = pairs_of(lambda x, y, z, core: (3 - x, y, z, core))


def send(block, pairs):
    return lax.ppermute(block, BOTH, pairs)


def row_live(count, first_row, height):
    rows = lax.broadcasted_iota(jnp.int32, (count, 1), 0) // W + first_row
    return jnp.where(jnp.logical_and(rows >= 0, rows < height), 1.0, 0.0)


def spread(stats_ref, cells, live, live_count):
    mean = jnp.sum(cells * live, axis=0, keepdims=True) / jnp.maximum(live_count, 1.0)
    centred = (cells - mean) * live
    both = jnp.concatenate([mean, jnp.sum(centred * centred, axis=0, keepdims=True)], axis=0)
    for i in range(16):
        stats_ref[i] = both


def stats_kernel(place_ref, image_ref, out_ref):
    first_row, height = place_ref[0], place_ref[1]
    count = (jnp.clip(height - first_row, 0, RP) * W).astype(F32)
    spread(out_ref, image_ref[...].astype(F32), row_live(TOK, first_row, height), count)


def half_kernel(place_ref, own_ref, out_ref, sem):
    start = pl.multiple_of(place_ref[2] * (9 * 80 - HALF), 16)
    copy = pltpu.make_async_copy(own_ref.at[pl.ds(start, HALF), :], out_ref, sem)
    copy.start()
    copy.wait()


GROUPS_OF_SLOTS = ((0, 4, 384), (4, 3, 256), (7, 1, 128))


def activate_kernel(
    place_ref, image_ref, above_ref, below_ref, affine_ref, *outs
):
    first_row, height = place_ref[0], place_ref[1]
    mean, gain, shift = affine_ref[0:1, :], affine_ref[1:2, :], affine_ref[2:3, :]
    channel = lax.broadcasted_iota(jnp.int32, (C, 128), 0)
    order = []
    for first_slot, slots, width in GROUPS_OF_SLOTS:
        wanted = []
        for at in range(0, width, 128):
            lane = lax.broadcasted_iota(jnp.int32, (1, 128), 1) + at
            source = jnp.full((1, 128), -1, jnp.int32)
            for s in range(slots):
                base = place_ref[3 + first_slot + s] * 80 - s * 80
                inside = jnp.logical_and(lane >= s * 80, lane < (s + 1) * 80)
                source = jnp.where(inside, lane + base, source)
            wanted.append(jnp.where(channel == source, 1.0, 0.0).astype(BF16))
        order.append(jnp.concatenate(wanted, axis=1))

    def put(at, count, block, row):
        live = row_live(count, row, height)
        v = (block.astype(F32) * live - mean) * gain + shift
        active = (v / (1.0 + jnp.exp(-v)) * live).astype(BF16)
        for matrix, out in zip(order, outs):
            out[at : at + count, :] = jnp.dot(
                active, matrix, preferred_element_type=F32
            ).astype(BF16)

    put(0, W, above_ref[...], first_row - 1)
    put(W, TOK, image_ref[...], first_row)
    put(W + TOK, W, below_ref[...], first_row + RP)


def weights_kernel(place_ref, wq_ref, wk_ref, wv_ref, wq_t_ref, wk_half_ref, wv_t_ref, turned):
    first_head = pl.ds(pl.multiple_of(place_ref[2] * HALF_C, HALF_C), HALF_C)
    turned[...] = wq_ref[...].T
    wq_t_ref[...] = turned[first_head, :]
    turned[...] = wv_ref[...].T
    wv_t_ref[...] = turned[first_head, :]
    turned[...] = wk_ref[...].T
    wk_half_ref[...] = turned[first_head, :].T


def conv_part(group, place_ref, first_ref, own_ref, mine, theirs, put):
    first_slot, slots, width = GROUPS_OF_SLOTS[group]
    remote = len(mine)
    pad = width - slots * 80

    def from_mine(i, row, rows):
        return mine[i][row : row + rows, :]

    def from_theirs(i, row, rows):
        return theirs[i][row : row + rows, :]

    def run(low, high):
        columns = lax.broadcasted_iota(jnp.int32, (TOK, 1), 0) % W

        def tap_weight(tap):
            pieces = [] if own_ref is None else [own_ref[80 * tap : 80 * tap + 80, :]]
            for i in range(remote):
                if tap <= 3:
                    pieces.append(low(i, 80 * tap, 80))
                elif tap >= 5:
                    pieces.append(high(i, 80 * tap - 352, 80))
                else:
                    pieces += [low(i, 320, 48), high(i, 16, 32)]
            return jnp.concatenate(pieces + [jnp.zeros((pad, C), BF16)], axis=0)

        total = None
        for dx in (0, 1, 2):
            part = None
            for dy in range(3):
                product = jnp.dot(
                    first_ref[dy * W : dy * W + TOK, :],
                    tap_weight(dy * 3 + dx),
                    preferred_element_type=F32,
                )
                part = product if part is None else part + product
            if dx == 0:
                part = jnp.where(columns == 0, 0.0, pltpu.roll(part, 1, 0))
            if dx == 2:
                part = jnp.where(columns == W - 1, 0.0, pltpu.roll(part, TOK - 1, 0))
            total = part if total is None else total + part
        put(total)

    pl.when(place_ref[2] == 0)(lambda: run(from_mine, from_theirs))
    pl.when(place_ref[2] != 0)(lambda: run(from_theirs, from_mine))


def conv_open_kernel(place_ref, first_ref, own_ref, a, b, c, d, e, f, out_ref):
    def put(total):
        out_ref[...] = total

    conv_part(0, place_ref, first_ref, own_ref, (a, b, c), (d, e, f), put)


def conv_more_kernel(place_ref, first_ref, a, b, c, d, e, f, held_ref, out_ref):
    def put(total):
        out_ref[...] = held_ref[...] + total

    conv_part(1, place_ref, first_ref, None, (a, b, c), (d, e, f), put)


def conv_close_kernel(
    place_ref, first_ref, a, theirs_ref, held_ref, image_ref, bias_ref, resid_ref, stats_ref
):
    first_row, height = place_ref[0], place_ref[1]
    live = row_live(TOK, first_row, height)

    def put(total):
        start = image_ref[...].astype(F32) * live
        conv = held_ref[...] + total
        resid_ref[...] = ((start + conv + bias_ref[...]) * live).astype(BF16)

    conv_part(2, place_ref, first_ref, None, (a,), (theirs_ref,), put)
    count = (jnp.clip(height - first_row, 0, RP) * W).astype(F32)
    spread(stats_ref, resid_ref[...].astype(F32), live, count)


def transposed(weight_t, block):
    return lax.dot_general(
        weight_t, block, (((1,), (1,)), ((), ())), preferred_element_type=F32
    ).astype(BF16)


def normalized(place_ref, affine_ref, row, block):
    mean, gain, shift = affine_ref[0:1, :], affine_ref[1:2, :], affine_ref[2:3, :]
    v = (block.astype(F32) - mean) * gain + shift
    return (v * row_live(TOK, row, place_ref[1])).astype(BF16)


def attend_block(place_ref, affine_ref, row, block, wk_ref, wv_ref, query_ref, top_of, put, mask=None):
    second = normalized(place_ref, affine_ref, row, block)
    keys = jnp.dot(second, wk_ref[...], preferred_element_type=F32).astype(BF16)
    values = transposed(wv_ref[...], second)
    tokens = lax.broadcasted_iota(jnp.int32, (VROWS - HEAD_DIM, TOK), 1)
    lines = lax.broadcasted_iota(jnp.int32, (VROWS - HEAD_DIM, TOK), 0)
    used = jnp.logical_and(lines == 0, tokens // W + row < place_ref[1])
    ones = jnp.where(used, 1.0, 0.0).astype(BF16)
    for h in range(MINE):
        pair = keys[:, h // 2 * 128 : min((h // 2 + 1) * 128, HALF_C)]
        s = jnp.dot(pair, query_ref[h, : pair.shape[1], :], preferred_element_type=F32)
        s = s * SCORE_SCALE
        if mask is not None:
            s = mask(s)
        weights = jnp.exp2(s - top_of(h, s)).astype(BF16)
        value = jnp.concatenate([values[h * HEAD_DIM : (h + 1) * HEAD_DIM], ones], axis=0)
        put(h, jnp.dot(value, weights, preferred_element_type=F32))


def open_kernel(place_ref, affine_ref, own_ref, other_ref, wq_ref, wk_ref, wv_ref, *refs):
    query_ref, acc_ref, top_ref = refs
    blocks = ((place_ref[2], own_ref), (place_ref[3], other_ref))
    for n, (row, ref) in enumerate(blocks):
        second = normalized(place_ref, affine_ref, row, ref[...])
        q = transposed(wq_ref[...], second)
        span = slice(n * TOK, (n + 1) * TOK)
        zero = jnp.zeros((HEAD_DIM, TOK), BF16)
        for h in range(MINE):
            here, there = h % 2 * HEAD_DIM, (h + 1) % 2 * HEAD_DIM
            query_ref[h, here : here + HEAD_DIM, span] = q[h * HEAD_DIM : (h + 1) * HEAD_DIM]
            query_ref[h, there : there + HEAD_DIM, span] = zero

    def top_of(h, s):
        top = jnp.max(s, axis=0, keepdims=True)
        top_ref[h] = jnp.broadcast_to(top, (8, QUERIES))
        return top

    def put(h, update):
        acc_ref[h] = update

    def add(h, update):
        acc_ref[h] += update

    for (row, ref), tops, store in zip(
        blocks, (top_of, lambda h, s: top_ref[h, 0:1, :]), (put, add)
    ):
        attend_block(
            place_ref, affine_ref, row, ref[...], wk_ref, wv_ref, query_ref, tops, store
        )


def attend_kernel(count, place_ref, affine_ref, query_ref, top_ref, wk_ref, wv_ref, *refs):
    sources, held_ref, acc_ref, blocks, sems = refs[:count], *refs[count:]
    for n, source in enumerate(sources):
        pltpu.make_async_copy(source, blocks.at[n], sems.at[n]).start()

    def put(h, update):
        acc_ref[h] += update

    def step(n, _):
        pltpu.make_async_copy(blocks.at[n], blocks.at[n], sems.at[n]).wait()
        attend_block(
            place_ref,
            affine_ref,
            place_ref[2 + n],
            blocks[n],
            wk_ref,
            wv_ref,
            query_ref,
            lambda h, s: top_ref[h, 0:1, :],
            put,
        )
        return 0

    acc_ref[...] = held_ref[...]
    lax.fori_loop(0, count, step, 0)


def close_kernel(
    place_ref, affine_ref, query_ref, top_ref, wk_ref, wv_ref, block_ref, held_ref, *refs
):
    blocks = refs[:16]
    mixed_ref, others_ref, acc_ref, highest, block, sem = refs[16:]

    def put(h, update):
        acc_ref[h] = held_ref[h] + update

    attend_block(
        place_ref,
        affine_ref,
        place_ref[2 + 15],
        block_ref[...],
        wk_ref,
        wv_ref,
        query_ref,
        lambda h, s: top_ref[h, 0:1, :],
        put,
    )
    far = jnp.zeros((1, QUERIES), F32)
    for h in range(MINE):
        total = acc_ref[h, HEAD_DIM : HEAD_DIM + 1, :]
        inside = jnp.logical_and(total > 2.0**-60, total < 2.0**100)
        far = jnp.maximum(far, jnp.where(inside, 0.0, 1.0))

    @pl.when(jnp.max(far) > 0.0)
    def _():
        highest[...] = jnp.full(highest.shape, -1e30, F32)
        acc_ref[...] = jnp.zeros(acc_ref.shape, F32)

        def step(n, _):
            for i, source in enumerate(blocks):

                @pl.when(n == i)
                def _():
                    copy = pltpu.make_async_copy(source, block, sem)
                    copy.start()
                    copy.wait()

            row = place_ref[2 + n]
            key_live = row_live(TOK, row, place_ref[1])

            def top_of(h, s):
                before = highest[h]
                after = jnp.maximum(before, jnp.max(s, axis=0, keepdims=True))
                highest[h] = after
                acc_ref[h] = acc_ref[h] * jnp.exp2(before - after)
                return after

            def add(h, update):
                acc_ref[h] += update

            def masked(s):
                return jnp.where(key_live > 0.0, s, -1e30)

            attend_block(
                place_ref,
                affine_ref,
                row,
                block[...],
                wk_ref,
                wv_ref,
                query_ref,
                top_of,
                add,
                masked,
            )
            return 0

        lax.fori_loop(0, 16, step, 0)

    for h in range(MINE):
        total = acc_ref[h, HEAD_DIM : HEAD_DIM + 1, :]
        total = jnp.where(total > 0.0, total, 1.0)
        mixed = (acc_ref[h, 0:HEAD_DIM, :] / total).astype(BF16)
        for n, ref in enumerate((mixed_ref, others_ref)):
            ref[h * HEAD_DIM : (h + 1) * HEAD_DIM, :] = mixed[:, n * TOK : (n + 1) * TOK]


def finish_kernel(place_ref, mixed_ref, other_ref, resid_ref, wo_ref, bias_ref, out_ref):
    core = place_ref[2]
    update = None
    for at, ref in ((core, mixed_ref), (1 - core, other_ref)):
        rows = pl.ds(pl.multiple_of(at * HALF_C, HALF_C), HALF_C)
        part = lax.dot_general(
            ref[...], wo_ref[rows, :], (((0,), (0,)), ((), ())), preferred_element_type=F32
        )
        update = part if update is None else update + part
    live = row_live(TOK, place_ref[0], place_ref[1])
    out_ref[...] = ((resid_ref[...].astype(F32) + update + bias_ref[...]) * live).astype(BF16)


def exchange(stats):
    return lax.all_to_all(stats, "patch", 0, 0, tiled=False)


def combine(everyone, height, gain, shift):
    rows = jnp.clip(height - RP * jnp.arange(16, dtype=jnp.int32), 0, RP)
    counts = (rows * W).astype(F32)[:, None, None]
    entries = (height * W * (C // GROUPS)).astype(F32)
    means = everyone[:, 0].reshape(16, GROUPS, C // GROUPS)
    squares = everyone[:, 1].reshape(16, GROUPS, C // GROUPS)
    mean = jnp.sum(means * counts, axis=(0, 2)) / entries
    apart = means - mean[None, :, None]
    spread = jnp.sum(squares + counts * apart * apart, axis=(0, 2)) / entries
    scale = lax.rsqrt(spread + 1e-05)
    wide = lambda v: jnp.broadcast_to(v[:, None], (GROUPS, C // GROUPS)).reshape(C)
    return jnp.stack([wide(mean), wide(scale) * gain, shift])


def per_device(
    images,
    heights,
    opening_scale_vector,
    opening_offset_vector,
    conv_weight,
    kernel_offset_vector,
    closing_scale_vector,
    closing_offset_vector,
    query_weight,
    key_weight,
    value_weight,
    out_weight,
    out_bias,
):
    image = images[0].reshape(TOK, C)
    height = heights[0]
    at_image = lax.axis_index("image")
    at_patch = lax.axis_index("patch")
    core = at_patch % 2
    first_row = at_patch * RP
    x_hi, y = at_image // 4, at_image % 4
    x_lo, z = at_patch // 8, at_patch // 2 % 4
    a_at = lambda by: x_hi * 4 + (y + by) % 4
    b_at = lambda by: (1 - x_hi) * 4 + (y + by) % 4
    place = jnp.stack(
        [first_row, height, core, at_image]
        + [a_at(3), a_at(1), b_at(0), a_at(2), b_at(3), b_at(1), b_at(2)]
    )

    own = conv_weight.reshape(9 * 80, C)
    half = pl.pallas_call(
        half_kernel,
        in_specs=[SMEM, HBM],
        out_specs=VMEM,
        out_shape=near((HALF, C), BF16),
        scratch_shapes=[pltpu.SemaphoreType.DMA],
        compiler_params=params(8),
    )(place, own)
    a_up = send(half, Y_UP)
    a_down = send(half, Y_DOWN)
    b_own = send(half, X_HI)

    stats = pl.pallas_call(
        stats_kernel,
        in_specs=[SMEM, VMEM],
        out_specs=VMEM,
        out_shape=shape((16, 2, C), F32),
        compiler_params=params(16),
    )(place, image)
    everyone = exchange(stats)
    a_up, a_down, b_own, bottom, top_row = lax.optimization_barrier(
        (a_up, a_down, b_own, image[TOK - W :], image[:W])
    )
    a_far = send(a_up, Y_UP)
    b_up = send(a_up, X_HI)
    b_down = send(b_own, Y_DOWN)
    up_pairs = [(g * 16 + i, g * 16 + i + 1) for g in range(8) for i in range(15)]
    above = send(bottom, up_pairs)
    below = send(top_row, [(b, a) for a, b in up_pairs])
    affine = combine(everyone, height, opening_scale_vector, opening_offset_vector)

    widths = [width for _, _, width in GROUPS_OF_SLOTS]
    first = pl.pallas_call(
        activate_kernel,
        in_specs=[SMEM] + [VMEM] * 4,
        out_specs=[VMEM] * 3,
        out_shape=[near((TOK + 2 * W, width), BF16) for width in widths],
        compiler_params=params(20),
        cost_estimate=cost(3),
    )(place, image, above, below, affine)
    widths = [width for _, _, width in GROUPS_OF_SLOTS]
    first = pl.pallas_call(
        activate_kernel,
        in_specs=[SMEM] + [VMEM] * 4,
        out_specs=[VMEM] * 3,
        out_shape=[near((TOK + 2 * W, width), BF16) for width in widths],
        compiler_params=params(20),
        cost_estimate=cost(3),
    )(place, image, above, below, affine)
    theirs_1 = [send(b, p) for b, p in zip((a_up, a_down, b_own), SIBLINGS)]
    mine_1, first = lax.optimization_barrier(([a_up, a_down, b_own], first))
    theirs_1 = [send(b, p) for b, p in zip(mine_1, SIBLINGS)]
    mine_2, theirs_1, first = lax.optimization_barrier(([a_far, b_up, b_down], theirs_1, first))
    b_far = send(mine_2[0], X_HI)
    theirs_2 = [send(b, p) for b, p in zip(mine_2, SIBLINGS)]
    conv = pl.pallas_call(
        conv_open_kernel,
        in_specs=[SMEM] + [VMEM] * 8,
        out_specs=VMEM,
        out_shape=near((TOK, C), F32),
        compiler_params=params(20),
        cost_estimate=cost(5),
    )(place, first[0], own, a_up, a_down, b_own, *theirs_1)
    conv, *qkv = lax.optimization_barrier((conv, query_weight, key_weight, value_weight))
    wq_t, wk, wv_t = pl.pallas_call(
        weights_kernel,
        in_specs=[SMEM] + [VMEM] * 3,
        out_specs=[VMEM] * 3,
        out_shape=[near(dims, BF16) for dims in ((HALF_C, C), (C, HALF_C), (HALF_C, C))],
        scratch_shapes=[pltpu.VMEM((C, C), BF16)],
        compiler_params=params(20),
        cost_estimate=cost(3),
    )(place, *qkv)
    b_far, theirs_2, conv, wq_t, wk, wv_t = lax.optimization_barrier(
        (b_far, theirs_2, conv, wq_t, wk, wv_t)
    )
    conv = pl.pallas_call(
        conv_more_kernel,
        in_specs=[SMEM] + [VMEM] * 8,
        out_specs=VMEM,
        out_shape=near((TOK, C), F32),
        input_output_aliases={8: 0},
        compiler_params=params(20),
        cost_estimate=cost(4),
    )(place, first[1], *mine_2, *theirs_2, conv)
    theirs_3 = send(b_far, SIBLING)
    resid, stats = pl.pallas_call(
        conv_close_kernel,
        in_specs=[SMEM] + [VMEM] * 6,
        out_specs=[VMEM, VMEM],
        out_shape=[near((TOK, C), BF16), shape((16, 2, C), F32)],
        compiler_params=params(20),
    )(place, first[2], b_far, theirs_3, conv, image, kernel_offset_vector[None, :])

    c_up = send(resid, Z_UP)
    c_down = send(resid, Z_DOWN)
    d_own = send(resid, X_LO)
    other_0 = send(resid, SIBLING)
    everyone = exchange(stats)
    c_up, c_down, d_own, other_0, everyone = lax.optimization_barrier(
        (c_up, c_down, d_own, other_0, everyone)
    )
    affine = combine(everyone, height, closing_scale_vector, closing_offset_vector)
    c_row = lambda by, at: (x_lo * 8 + (z + by) % 4 * 2 + at) * RP
    d_row = lambda by, at: ((1 - x_lo) * 8 + (z + by) % 4 * 2 + at) * RP
    rows_of = lambda at: [
        [c_row(0, at)],
        [c_row(3, at), c_row(1, at), d_row(0, at)],
        [c_row(2, at), d_row(3, at), d_row(1, at)],
        [d_row(2, at)],
    ]
    mine, theirs = rows_of(core), rows_of(1 - core)

    def rows_place(rows):
        return jnp.stack([first_row, height] + rows)

    acc_shape = (MINE, VROWS, QUERIES)

    def attend(blocks, rows, acc):
        return pl.pallas_call(
            functools.partial(attend_kernel, len(blocks)),
            in_specs=[SMEM] + [VMEM] * 5 + [ANY] * len(blocks) + [VMEM],
            out_specs=VMEM,
            out_shape=near(acc_shape, F32),
            input_output_aliases={6 + len(blocks): 0},
            scratch_shapes=[
                pltpu.VMEM((len(blocks), TOK, C), BF16),
                pltpu.SemaphoreType.DMA((len(blocks),)),
            ],
            compiler_params=params(28),
            cost_estimate=cost(3.5 * len(rows)),
        )(rows_place(rows), affine, query, top, wk, wv_t, *blocks, acc)

    query, acc, top = pl.pallas_call(
        open_kernel,
        in_specs=[SMEM] + [VMEM] * 6,
        out_specs=[VMEM] * 3,
        out_shape=[
            near((MINE, 2 * HEAD_DIM, QUERIES), BF16),
            near(acc_shape, F32),
            near((MINE, 8, QUERIES), F32),
        ],
        compiler_params=params(28),
        cost_estimate=cost(0),
    )(rows_place(mine[0] + theirs[0]), affine, resid, other_0, wq_t, wk, wv_t)

    c_far = send(c_up, Z_UP)
    d_up = send(c_up, X_LO)
    d_down = send(d_own, Z_DOWN)
    mine_1 = [c_up, c_down, d_own]
    other_1 = [send(c_up, SIBLING)]
    acc = attend(mine_1, mine[1], acc)
    late, other_1, acc = lax.optimization_barrier((mine_1[1:], other_1, acc))
    other_1 += [send(block, pairs) for block, pairs in zip(late, SIBLINGS)]
    acc = attend(other_1[:1], theirs[1][:1], acc)
    c_far, d_up, d_down, other_1, acc = lax.optimization_barrier(
        (c_far, d_up, d_down, other_1, acc)
    )
    last = send(c_far, X_LO)
    mine_2 = [c_far, d_up, d_down]
    other_2 = [send(block, pairs) for block, pairs in zip(mine_2, SIBLINGS)]
    acc = attend(other_1[1:], theirs[1][1:], acc)
    acc = attend(mine_2, mine[2], acc)
    last, other_2, acc = lax.optimization_barrier((last, other_2, acc))
    other_3 = send(last, SIBLING)
    acc = attend(other_2 + [last], theirs[2] + mine[3], acc)
    other_3, acc = lax.optimization_barrier((other_3, acc))
    blocks = [resid, other_0] + mine_1 + other_1 + mine_2 + other_2 + [last, other_3]
    order = mine[0] + theirs[0] + mine[1] + theirs[1] + mine[2] + theirs[2] + mine[3] + theirs[3]
    mixed, others = pl.pallas_call(
        close_kernel,
        in_specs=[SMEM] + [VMEM] * 7 + [ANY] * 16,
        out_specs=[VMEM] * 2,
        out_shape=[near((HALF_C, TOK), BF16)] * 2,
        scratch_shapes=[
            pltpu.VMEM(acc_shape, F32),
            pltpu.VMEM((MINE, 1, QUERIES), F32),
            pltpu.VMEM((TOK, C), BF16),
            pltpu.SemaphoreType.DMA,
        ],
        compiler_params=params(28),
        cost_estimate=cost(5),
    )(rows_place(order), affine, query, top, wk, wv_t, other_3, acc, *blocks)
    other = send(others, SIBLING)
    out = pl.pallas_call(
        finish_kernel,
        in_specs=[SMEM] + [VMEM] * 5,
        out_specs=VMEM,
        out_shape=shape((TOK, C), BF16),
        compiler_params=params(20),
    )(place, mixed, other, resid, out_weight, out_bias[None, :])
    return out.reshape(1, RP, W, C)


def solution(mesh):
    in_specs = (
        P("image", "patch", None, None),
        P("image"),
        P(),
        P(),
        P(None, None, "image", None),
        P(),
        P(),
        P(),
        P(),
        P(),
        P(),
        P(),
        P(),
    )
    out_specs = P("image", "patch", None, None)
    return jax.shard_map(
        per_device, mesh=mesh, in_specs=in_specs, out_specs=out_specs, check_vma=False
    )
```

```python
import functools

import jax
import jax.numpy as jnp
from jax import lax
from jax.experimental import pallas as pl
from jax.experimental.pallas import tpu as pltpu
from jax.sharding import PartitionSpec as P

HEAD_DIM = 64
GROUPS = 32
C = 640
W = 64
RP = 8
TOK = RP * W
HEADS = C // HEAD_DIM
VROWS = 80
MINE = HEADS // 2
HALF_C = C // 2
QUERIES = 2 * TOK
HALF = 368
BOTH = ("image", "patch")
SCORE_SCALE = HEAD_DIM**-0.5 * 1.4426950408889634
VMEM = pl.BlockSpec(memory_space=pltpu.VMEM)
SMEM = pl.BlockSpec(memory_space=pltpu.SMEM)
ANY = pl.BlockSpec(memory_space=pl.ANY)
HBM = pl.BlockSpec(memory_space=pltpu.HBM)
F32 = jnp.float32
BF16 = jnp.bfloat16


def params(mib):
    return pltpu.CompilerParams(vmem_limit_bytes=mib << 20)


def cost(microseconds):
    return pl.CostEstimate(
        flops=int(microseconds * 1e9), bytes_accessed=int(microseconds * 3e6), transcendentals=0
    )


def near(dims, kind):
    return pltpu.VMEM(dims, kind)


def shape(dims, kind):
    return jax.ShapeDtypeStruct(dims, kind)


def pairs_of(move):
    pairs = []
    for x in range(4):
        for y in range(4):
            for z in range(4):
                for core in range(2):
                    ends = []
                    for a, b, c, d in ((x, y, z, core), move(x, y, z, core)):
                        a, b, c = a % 4, b % 4, c % 4
                        ends.append((a // 2 * 4 + b) * 16 + a % 2 * 8 + c * 2 + d)
                    pairs.append(tuple(ends))
    return pairs


SIBLING = pairs_of(lambda x, y, z, core: (x, y, z, 1 - core))
SIBLINGS = [SIBLING, SIBLING[1:] + SIBLING[:1], SIBLING[2:] + SIBLING[:2]]
Y_UP = pairs_of(lambda x, y, z, core: (x, y + 1, z, core))
Y_DOWN = pairs_of(lambda x, y, z, core: (x, y - 1, z, core))
Z_UP = pairs_of(lambda x, y, z, core: (x, y, z + 1, core))
Z_DOWN = pairs_of(lambda x, y, z, core: (x, y, z - 1, core))
X_LO = pairs_of(lambda x, y, z, core: (x ^ 1, y, z, core))
X_HI = pairs_of(lambda x, y, z, core: (3 - x, y, z, core))


def send(block, pairs):
    return lax.ppermute(block, BOTH, pairs)


def row_live(count, first_row, height):
    rows = lax.broadcasted_iota(jnp.int32, (count, 1), 0) // W + first_row
    return jnp.where(jnp.logical_and(rows >= 0, rows < height), 1.0, 0.0)


def spread(stats_ref, cells, live, live_count):
    mean = jnp.sum(cells * live, axis=0, keepdims=True) / jnp.maximum(live_count, 1.0)
    centred = (cells - mean) * live
    both = jnp.concatenate([mean, jnp.sum(centred * centred, axis=0, keepdims=True)], axis=0)
    for i in range(16):
        stats_ref[i] = both


def stats_kernel(place_ref, image_ref, out_ref):
    first_row, height = place_ref[0], place_ref[1]
    count = (jnp.clip(height - first_row, 0, RP) * W).astype(F32)
    spread(out_ref, image_ref[...].astype(F32), row_live(TOK, first_row, height), count)


def half_kernel(place_ref, own_ref, out_ref, sem):
    start = pl.multiple_of(place_ref[2] * (9 * 80 - HALF), 16)
    copy = pltpu.make_async_copy(own_ref.at[pl.ds(start, HALF), :], out_ref, sem)
    copy.start()
    copy.wait()


GROUPS_OF_SLOTS = ((0, 4, 384), (4, 3, 256), (7, 1, 128))


def activate_kernel(
    place_ref, image_ref, above_ref, below_ref, affine_ref, *outs
):
    first_row, height = place_ref[0], place_ref[1]
    mean, gain, shift = affine_ref[0:1, :], affine_ref[1:2, :], affine_ref[2:3, :]
    channel = lax.broadcasted_iota(jnp.int32, (C, 128), 0)
    order = []
    for first_slot, slots, width in GROUPS_OF_SLOTS:
        wanted = []
        for at in range(0, width, 128):
            lane = lax.broadcasted_iota(jnp.int32, (1, 128), 1) + at
            source = jnp.full((1, 128), -1, jnp.int32)
            for s in range(slots):
                base = place_ref[3 + first_slot + s] * 80 - s * 80
                inside = jnp.logical_and(lane >= s * 80, lane < (s + 1) * 80)
                source = jnp.where(inside, lane + base, source)
            wanted.append(jnp.where(channel == source, 1.0, 0.0).astype(BF16))
        order.append(jnp.concatenate(wanted, axis=1))

    def put(at, count, block, row):
        live = row_live(count, row, height)
        v = (block.astype(F32) * live - mean) * gain + shift
        active = (v / (1.0 + jnp.exp(-v)) * live).astype(BF16)
        for matrix, out in zip(order, outs):
            out[at : at + count, :] = jnp.dot(
                active, matrix, preferred_element_type=F32
            ).astype(BF16)

    put(0, W, above_ref[...], first_row - 1)
    put(W, TOK, image_ref[...], first_row)
    put(W + TOK, W, below_ref[...], first_row + RP)


def weights_kernel(place_ref, wq_ref, wk_ref, wv_ref, wq_t_ref, wk_half_ref, wv_t_ref, turned):
    first_head = pl.ds(pl.multiple_of(place_ref[2] * HALF_C, HALF_C), HALF_C)
    turned[...] = wq_ref[...].T
    wq_t_ref[...] = turned[first_head, :]
    turned[...] = wv_ref[...].T
    wv_t_ref[...] = turned[first_head, :]
    turned[...] = wk_ref[...].T
    wk_half_ref[...] = turned[first_head, :].T


def conv_part(group, place_ref, first_ref, own_ref, mine, theirs, put):
    first_slot, slots, width = GROUPS_OF_SLOTS[group]
    remote = len(mine)
    pad = width - slots * 80

    def from_mine(i, row, rows):
        return mine[i][row : row + rows, :]

    def from_theirs(i, row, rows):
        return theirs[i][row : row + rows, :]

    def run(low, high):
        columns = lax.broadcasted_iota(jnp.int32, (TOK, 1), 0) % W

        def tap_weight(tap):
            pieces = [] if own_ref is None else [own_ref[80 * tap : 80 * tap + 80, :]]
            for i in range(remote):
                if tap <= 3:
                    pieces.append(low(i, 80 * tap, 80))
                elif tap >= 5:
                    pieces.append(high(i, 80 * tap - 352, 80))
                else:
                    pieces += [low(i, 320, 48), high(i, 16, 32)]
            return jnp.concatenate(pieces + [jnp.zeros((pad, C), BF16)], axis=0)

        total = None
        for dx in (0, 1, 2):
            part = None
            for dy in range(3):
                product = jnp.dot(
                    first_ref[dy * W : dy * W + TOK, :],
                    tap_weight(dy * 3 + dx),
                    preferred_element_type=F32,
                )
                part = product if part is None else part + product
            if dx == 0:
                part = jnp.where(columns == 0, 0.0, pltpu.roll(part, 1, 0))
            if dx == 2:
                part = jnp.where(columns == W - 1, 0.0, pltpu.roll(part, TOK - 1, 0))
            total = part if total is None else total + part
        put(total)

    pl.when(place_ref[2] == 0)(lambda: run(from_mine, from_theirs))
    pl.when(place_ref[2] != 0)(lambda: run(from_theirs, from_mine))


def conv_open_kernel(place_ref, first_ref, own_ref, a, b, c, d, e, f, out_ref):
    def put(total):
        out_ref[...] = total

    conv_part(0, place_ref, first_ref, own_ref, (a, b, c), (d, e, f), put)


def conv_more_kernel(place_ref, first_ref, a, b, c, d, e, f, held_ref, out_ref):
    def put(total):
        out_ref[...] = held_ref[...] + total

    conv_part(1, place_ref, first_ref, None, (a, b, c), (d, e, f), put)


def conv_close_kernel(
    place_ref, first_ref, a, theirs_ref, held_ref, image_ref, bias_ref, resid_ref, stats_ref
):
    first_row, height = place_ref[0], place_ref[1]
    live = row_live(TOK, first_row, height)

    def put(total):
        start = image_ref[...].astype(F32) * live
        conv = held_ref[...] + total
        resid_ref[...] = ((start + conv + bias_ref[...]) * live).astype(BF16)

    conv_part(2, place_ref, first_ref, None, (a,), (theirs_ref,), put)
    count = (jnp.clip(height - first_row, 0, RP) * W).astype(F32)
    spread(stats_ref, resid_ref[...].astype(F32), live, count)


def transposed(weight_t, block):
    return lax.dot_general(
        weight_t, block, (((1,), (1,)), ((), ())), preferred_element_type=F32
    ).astype(BF16)


def normalized(place_ref, affine_ref, row, block):
    mean, gain, shift = affine_ref[0:1, :], affine_ref[1:2, :], affine_ref[2:3, :]
    v = (block.astype(F32) - mean) * gain + shift
    return (v * row_live(TOK, row, place_ref[1])).astype(BF16)


def project_pair(place_ref, affine_ref, blocks, wk_ref, wv_ref, keys_ref, values_ref):
    second, ones = [], []
    for n, ref in enumerate(blocks):
        row = place_ref[2 + n]
        second.append(normalized(place_ref, affine_ref, row, ref[...]))
        ones.append(count_row(TOK, row, place_ref[1]))
    second = jnp.concatenate(second, axis=0)
    keys_ref[:, 0:HALF_C] = jnp.dot(second, wk_ref[...], preferred_element_type=F32).astype(BF16)
    keys_ref[:, HALF_C:] = jnp.zeros((QUERIES, 3 * 128 - HALF_C), BF16)
    values_ref[...] = transposed(wv_ref[...], second)
    return jnp.concatenate(ones, axis=1)


def count_row(count, first_row, height):
    tokens = lax.broadcasted_iota(jnp.int32, (VROWS - HEAD_DIM, count), 1)
    lines = lax.broadcasted_iota(jnp.int32, (VROWS - HEAD_DIM, count), 0)
    used = jnp.logical_and(lines == 0, tokens // W + first_row < height)
    return jnp.where(used, 1.0, 0.0).astype(BF16)


def scores_of(keys, query_ref, h):
    return jnp.dot(keys, query_ref[h], preferred_element_type=F32) * SCORE_SCALE


def attend_exactly(place_ref, query_ref, held, acc_ref, top_ref, keys_ref, values_ref):
    parts = QUERIES // 128

    def start(h, _):
        acc_ref[h] = jnp.zeros((VROWS, QUERIES), F32) if held[0] is None else held[0][h]
        return 0

    def step(i, _):
        h, part = i // parts, i % parts
        row = place_ref[2 + part // 4] + part % 4 * 2
        at = pl.ds(pl.multiple_of(part * 128, 128), 128)
        pair = pl.ds(pl.multiple_of(h // 2 * 128, 128), 128)
        shut = row_live(128, row, place_ref[1]) * 1e30 - 1e30
        s = scores_of(keys_ref[at, pair], query_ref, h) + shut
        before = top_ref[h, 0:1, :]
        top = jnp.maximum(before, jnp.max(s, axis=0, keepdims=True))
        head = pl.ds(pl.multiple_of(h * HEAD_DIM, HEAD_DIM), HEAD_DIM)
        value = jnp.concatenate(
            [values_ref[head, at], count_row(128, row, place_ref[1])], axis=0
        )
        weights = jnp.exp2(s - top).astype(BF16)
        update = jnp.dot(value, weights, preferred_element_type=F32)
        acc_ref[h] = acc_ref[h] * jnp.exp2(before - top) + update
        top_ref[h] = jnp.broadcast_to(top, (8, QUERIES))
        return 0

    lax.fori_loop(0, MINE, start, 0)
    lax.fori_loop(0, MINE * parts, step, 0)


def attend_pair(
    place_ref, affine_ref, blocks, wk_ref, wv_ref, query_ref, held, acc_ref, top_ref, scratch
):
    keys_ref, values_ref = scratch
    ones = project_pair(
        place_ref, affine_ref, blocks, wk_ref, wv_ref, keys_ref, values_ref
    )
    far = jnp.zeros((1, QUERIES), F32)
    for h in range(MINE):
        pair = keys_ref[:, h // 2 * 128 : (h // 2 + 1) * 128]
        weights = jnp.exp2(scores_of(pair, query_ref, h) - held[1][h, 0:1, :]).astype(BF16)
        value = jnp.concatenate(
            [values_ref[h * HEAD_DIM : (h + 1) * HEAD_DIM, :], ones], axis=0
        )
        update = jnp.dot(value, weights, preferred_element_type=F32)
        inside = update[HEAD_DIM : HEAD_DIM + 1, :] < 2.0**100
        far = jnp.maximum(far, jnp.where(inside, 0.0, 1.0))
        acc_ref[h] = update if held[0] is None else held[0][h] + update
    top_ref[...] = held[1][...]

    @pl.when(jnp.max(far) > 0.0)
    def _():
        attend_exactly(place_ref, query_ref, held, acc_ref, top_ref, keys_ref, values_ref)


def open_kernel(place_ref, affine_ref, own_ref, other_ref, wq_ref, wk_ref, wv_ref, *refs):
    query_ref, acc_ref, top_ref, first_ref, *scratch = refs
    blocks = (own_ref, other_ref)
    for n, ref in enumerate(blocks):
        q = transposed(wq_ref[...], normalized(place_ref, affine_ref, place_ref[2 + n], ref[...]))
        span = slice(n * TOK, (n + 1) * TOK)
        zero = jnp.zeros((HEAD_DIM, TOK), BF16)
        for h in range(MINE):
            here, there = h % 2 * HEAD_DIM, (h + 1) % 2 * HEAD_DIM
            query_ref[h, here : here + HEAD_DIM, span] = q[h * HEAD_DIM : (h + 1) * HEAD_DIM]
            query_ref[h, there : there + HEAD_DIM, span] = zero
    opening, shut = [], []
    for n, ref in enumerate(blocks):
        live = row_live(W, place_ref[2 + n], place_ref[1])
        mean, gain, shift = affine_ref[0:1, :], affine_ref[1:2, :], affine_ref[2:3, :]
        v = (ref[0:W, :].astype(F32) - mean) * gain + shift
        opening.append((v * live).astype(BF16))
        shut.append(live * 1e30 - 1e30)
    keys = jnp.dot(jnp.concatenate(opening, axis=0), wk_ref[...], preferred_element_type=F32)
    keys = jnp.concatenate([keys, jnp.zeros((2 * W, 3 * 128 - HALF_C), F32)], axis=1).astype(BF16)
    shut = jnp.concatenate(shut, axis=0)
    for h in range(MINE):
        pair = keys[:, h // 2 * 128 : (h // 2 + 1) * 128]
        top = jnp.max(scores_of(pair, query_ref, h) + shut, axis=0, keepdims=True)
        top = jnp.where(top < -1e29, 0.0, top)
        first_ref[h] = jnp.broadcast_to(top, (8, QUERIES))
    attend_pair(
        place_ref,
        affine_ref,
        blocks,
        wk_ref,
        wv_ref,
        query_ref,
        (None, first_ref),
        acc_ref,
        top_ref,
        scratch,
    )


def attend_kernel(
    place_ref, affine_ref, query_ref, wk_ref, wv_ref, a, b, held_ref, before_ref, *refs
):
    acc_ref, top_ref, *scratch = refs
    held = held_ref, before_ref
    attend_pair(
        place_ref, affine_ref, (a, b), wk_ref, wv_ref, query_ref, held, acc_ref, top_ref, scratch
    )


def close_kernel(
    place_ref, affine_ref, query_ref, wk_ref, wv_ref, a, b, held_ref, before_ref, *refs
):
    mixed_ref, others_ref, acc_ref, top_ref, *scratch = refs
    held = held_ref, before_ref
    attend_pair(
        place_ref, affine_ref, (a, b), wk_ref, wv_ref, query_ref, held, acc_ref, top_ref, scratch
    )
    for h in range(MINE):
        mixed = acc_ref[h, 0:HEAD_DIM, :] / acc_ref[h, HEAD_DIM : HEAD_DIM + 1, :]
        mixed = mixed.astype(BF16)
        for n, ref in enumerate((mixed_ref, others_ref)):
            ref[h * HEAD_DIM : (h + 1) * HEAD_DIM, :] = mixed[:, n * TOK : (n + 1) * TOK]


def finish_kernel(place_ref, mixed_ref, other_ref, resid_ref, wo_ref, bias_ref, out_ref):
    core = place_ref[2]
    update = None
    for at, ref in ((core, mixed_ref), (1 - core, other_ref)):
        rows = pl.ds(pl.multiple_of(at * HALF_C, HALF_C), HALF_C)
        part = lax.dot_general(
            ref[...], wo_ref[rows, :], (((0,), (0,)), ((), ())), preferred_element_type=F32
        )
        update = part if update is None else update + part
    live = row_live(TOK, place_ref[0], place_ref[1])
    out_ref[...] = ((resid_ref[...].astype(F32) + update + bias_ref[...]) * live).astype(BF16)


def exchange(stats):
    return lax.all_to_all(stats, "patch", 0, 0, tiled=False)


def combine_kernel(place_ref, everyone_ref, gain_ref, shift_ref, out_ref):
    height = place_ref[1]
    patch = lax.broadcasted_iota(jnp.int32, (16, 1), 0)
    counts = (jnp.clip(height - RP * patch, 0, RP) * W).astype(F32)
    entries = (height * W * (C // GROUPS)).astype(F32)
    channel = lax.broadcasted_iota(jnp.int32, (C, 128), 0)
    group = lax.broadcasted_iota(jnp.int32, (C, 128), 1)
    member = jnp.where(channel // (C // GROUPS) == group, 1.0, 0.0)

    def over_group(line):
        lines = jnp.broadcast_to(line, (8, C))
        return lax.dot_general(
            lines,
            member,
            (((1,), (0,)), ((), ())),
            precision=lax.Precision.HIGHEST,
            preferred_element_type=F32,
        )

    def widened(groups):
        return lax.dot_general(
            groups,
            member,
            (((1,), (1,)), ((), ())),
            precision=lax.Precision.HIGHEST,
            preferred_element_type=F32,
        )

    means, squares = everyone_ref[:, 0, :], everyone_ref[:, 1, :]
    mean = widened(over_group(jnp.sum(means * counts, axis=0, keepdims=True)) / entries)
    apart = means - mean[0:1, :]
    spread_sum = jnp.sum(squares + counts * apart * apart, axis=0, keepdims=True)
    scale = widened(lax.rsqrt(over_group(spread_sum) / entries + 1e-05))
    out_ref[0:1, :] = mean[0:1, :]
    out_ref[1:2, :] = scale[0:1, :] * gain_ref[...]
    out_ref[2:3, :] = shift_ref[...]


def combine(place, everyone, gain, shift):
    return pl.pallas_call(
        combine_kernel,
        in_specs=[SMEM] + [VMEM] * 3,
        out_specs=VMEM,
        out_shape=near((3, C), F32),
        compiler_params=params(16),
    )(place, everyone, gain[None, :], shift[None, :])


def per_device(
    images,
    heights,
    opening_scale_vector,
    opening_offset_vector,
    conv_weight,
    kernel_offset_vector,
    closing_scale_vector,
    closing_offset_vector,
    query_weight,
    key_weight,
    value_weight,
    out_weight,
    out_bias,
):
    image = images[0].reshape(TOK, C)
    height = heights[0]
    at_image = lax.axis_index("image")
    at_patch = lax.axis_index("patch")
    core = at_patch % 2
    first_row = at_patch * RP
    x_hi, y = at_image // 4, at_image % 4
    x_lo, z = at_patch // 8, at_patch // 2 % 4
    a_at = lambda by: x_hi * 4 + (y + by) % 4
    b_at = lambda by: (1 - x_hi) * 4 + (y + by) % 4
    place = jnp.stack(
        [first_row, height, core, at_image]
        + [a_at(3), a_at(1), b_at(0), a_at(2), b_at(3), b_at(1), b_at(2)]
    )

    own = conv_weight.reshape(9 * 80, C)
    half = pl.pallas_call(
        half_kernel,
        in_specs=[SMEM, HBM],
        out_specs=VMEM,
        out_shape=near((HALF, C), BF16),
        scratch_shapes=[pltpu.SemaphoreType.DMA],
        compiler_params=params(8),
    )(place, own)
    a_up = send(half, Y_UP)
    a_down = send(half, Y_DOWN)
    b_own = send(half, X_HI)

    stats = pl.pallas_call(
        stats_kernel,
        in_specs=[SMEM, VMEM],
        out_specs=VMEM,
        out_shape=shape((16, 2, C), F32),
        compiler_params=params(16),
    )(place, image)
    everyone = exchange(stats)
    a_up, a_down, b_own, everyone, bottom, top_row = lax.optimization_barrier(
        (a_up, a_down, b_own, everyone, image[TOK - W :], image[:W])
    )
    a_far = send(a_up, Y_UP)
    b_up = send(a_up, X_HI)
    b_down = send(b_own, Y_DOWN)
    up_pairs = [(g * 16 + i, g * 16 + i + 1) for g in range(8) for i in range(15)]
    above = send(bottom, up_pairs)
    below = send(top_row, [(b, a) for a, b in up_pairs])
    affine = combine(place, everyone, opening_scale_vector, opening_offset_vector)

    widths = [width for _, _, width in GROUPS_OF_SLOTS]
    first = pl.pallas_call(
        activate_kernel,
        in_specs=[SMEM] + [VMEM] * 4,
        out_specs=[VMEM] * 3,
        out_shape=[near((TOK + 2 * W, width), BF16) for width in widths],
        compiler_params=params(20),
        cost_estimate=cost(3),
    )(place, image, above, below, affine)
    widths = [width for _, _, width in GROUPS_OF_SLOTS]
    first = pl.pallas_call(
        activate_kernel,
        in_specs=[SMEM] + [VMEM] * 4,
        out_specs=[VMEM] * 3,
        out_shape=[near((TOK + 2 * W, width), BF16) for width in widths],
        compiler_params=params(20),
        cost_estimate=cost(3),
    )(place, image, above, below, affine)
    theirs_1 = [send(b, p) for b, p in zip((a_up, a_down, b_own), SIBLINGS)]
    mine_1, first = lax.optimization_barrier(([a_up, a_down, b_own], first))
    theirs_1 = [send(b, p) for b, p in zip(mine_1, SIBLINGS)]
    mine_2, theirs_1, first = lax.optimization_barrier(([a_far, b_up, b_down], theirs_1, first))
    b_far = send(mine_2[0], X_HI)
    theirs_2 = [send(b, p) for b, p in zip(mine_2, SIBLINGS)]
    conv = pl.pallas_call(
        conv_open_kernel,
        in_specs=[SMEM] + [VMEM] * 8,
        out_specs=VMEM,
        out_shape=near((TOK, C), F32),
        compiler_params=params(20),
        cost_estimate=cost(5),
    )(place, first[0], own, a_up, a_down, b_own, *theirs_1)
    conv, *qkv = lax.optimization_barrier((conv, query_weight, key_weight, value_weight))
    wq_t, wk, wv_t = pl.pallas_call(
        weights_kernel,
        in_specs=[SMEM] + [VMEM] * 3,
        out_specs=[VMEM] * 3,
        out_shape=[near(dims, BF16) for dims in ((HALF_C, C), (C, HALF_C), (HALF_C, C))],
        scratch_shapes=[pltpu.VMEM((C, C), BF16)],
        compiler_params=params(20),
        cost_estimate=cost(3),
    )(place, *qkv)
    b_far, theirs_2, conv, wq_t, wk, wv_t = lax.optimization_barrier(
        (b_far, theirs_2, conv, wq_t, wk, wv_t)
    )
    conv = pl.pallas_call(
        conv_more_kernel,
        in_specs=[SMEM] + [VMEM] * 8,
        out_specs=VMEM,
        out_shape=near((TOK, C), F32),
        input_output_aliases={8: 0},
        compiler_params=params(20),
        cost_estimate=cost(4),
    )(place, first[1], *mine_2, *theirs_2, conv)
    theirs_3 = send(b_far, SIBLING)
    resid, stats = pl.pallas_call(
        conv_close_kernel,
        in_specs=[SMEM] + [VMEM] * 6,
        out_specs=[VMEM, VMEM],
        out_shape=[near((TOK, C), BF16), shape((16, 2, C), F32)],
        compiler_params=params(20),
    )(place, first[2], b_far, theirs_3, conv, image, kernel_offset_vector[None, :])

    other_0 = send(resid, SIBLING)
    everyone = exchange(stats)
    mine_0, other_0, everyone = lax.optimization_barrier((resid, other_0, everyone))
    c_up = send(mine_0, Z_UP)
    c_down = send(mine_0, Z_DOWN)
    d_own = send(mine_0, X_LO)
    affine = combine(place, everyone, closing_scale_vector, closing_offset_vector)
    c_row = lambda by, at: (x_lo * 8 + (z + by) % 4 * 2 + at) * RP
    d_row = lambda by, at: ((1 - x_lo) * 8 + (z + by) % 4 * 2 + at) * RP
    rows_of = lambda at: [
        [c_row(0, at)],
        [c_row(3, at), c_row(1, at), d_row(0, at)],
        [c_row(2, at), d_row(3, at), d_row(1, at)],
        [d_row(2, at)],
    ]
    mine, theirs = rows_of(core), rows_of(1 - core)

    def rows_place(rows):
        return jnp.stack([first_row, height] + rows)

    acc_shape = (MINE, VROWS, QUERIES)

    top_shape = (MINE, 8, QUERIES)
    pair_scratch = [pltpu.VMEM((QUERIES, 3 * 128), BF16), pltpu.VMEM((HALF_C, QUERIES), BF16)]

    def attend(blocks, rows, state):
        return pl.pallas_call(
            attend_kernel,
            in_specs=[SMEM] + [VMEM] * 8,
            out_specs=[VMEM] * 2,
            out_shape=[near(acc_shape, F32), near(top_shape, F32)],
            scratch_shapes=pair_scratch,
            compiler_params=params(24),
        )(rows_place(rows), affine, query, wk, wv_t, *blocks, *state)

    def held_until(blocks, state):
        return lax.optimization_barrier((blocks, state))

    query, *state = pl.pallas_call(
        open_kernel,
        in_specs=[SMEM] + [VMEM] * 6,
        out_specs=[VMEM] * 3,
        out_shape=[
            near((MINE, 2 * HEAD_DIM, QUERIES), BF16),
            near(acc_shape, F32),
            near(top_shape, F32),
        ],
        scratch_shapes=[pltpu.VMEM(top_shape, F32)] + pair_scratch,
        compiler_params=params(24),
    )(rows_place(mine[0] + theirs[0]), affine, resid, other_0, wq_t, wk, wv_t)

    mine_1, state = held_until([c_up, c_down, d_own], state)
    c_far = send(mine_1[0], Z_UP)
    d_up = send(mine_1[0], X_LO)
    d_down = send(mine_1[2], Z_DOWN)
    other_1 = [send(mine_1[0], SIBLING)]
    state = attend(mine_1[:2], mine[1][:2], state)
    (late, other_1), state = held_until((mine_1[1:], other_1), state)
    other_1 += [send(block, pairs) for block, pairs in zip(late, SIBLINGS)]
    state = attend([late[1], other_1[0]], mine[1][2:] + theirs[1][:1], state)
    state = attend(other_1[1:], theirs[1][1:], state)

    mine_2, state = held_until([c_far, d_up, d_down], state)
    last = send(mine_2[0], X_LO)
    other_2 = [send(block, pairs) for block, pairs in zip(mine_2, SIBLINGS)]
    state = attend(mine_2[:2], mine[2][:2], state)
    state = attend([mine_2[2], other_2[0]], mine[2][2:] + theirs[2][:1], state)
    (last, other_2), state = held_until((last, other_2), state)
    other_3 = send(last, SIBLING)
    state = attend(other_2[1:], theirs[2][1:], state)
    other_3, state = held_until(other_3, state)

    mixed, others = pl.pallas_call(
        close_kernel,
        in_specs=[SMEM] + [VMEM] * 8,
        out_specs=[VMEM] * 2,
        out_shape=[near((HALF_C, TOK), BF16)] * 2,
        scratch_shapes=[pltpu.VMEM(acc_shape, F32), pltpu.VMEM(top_shape, F32)] + pair_scratch,
        compiler_params=params(24),
    )(rows_place(mine[3] + theirs[3]), affine, query, wk, wv_t, last, other_3, *state)
    other = send(others, SIBLING)
    out = pl.pallas_call(
        finish_kernel,
        in_specs=[SMEM] + [VMEM] * 5,
        out_specs=VMEM,
        out_shape=shape((TOK, C), BF16),
        compiler_params=params(20),
    )(place, mixed, other, resid, out_weight, out_bias[None, :])
    return out.reshape(1, RP, W, C)


def solution(mesh):
    in_specs = (
        P("image", "patch", None, None),
        P("image"),
        P(),
        P(),
        P(None, None, "image", None),
        P(),
        P(),
        P(),
        P(),
        P(),
        P(),
        P(),
        P(),
    )
    out_specs = P("image", "patch", None, None)
    return jax.shard_map(
        per_device, mesh=mesh, in_specs=in_specs, out_specs=out_specs, check_vma=False
    )
```

```python
import functools

import jax
import jax.numpy as jnp
from jax import lax
from jax.experimental import pallas as pl
from jax.experimental.pallas import tpu as pltpu
from jax.sharding import PartitionSpec as P

HEAD_DIM = 64
GROUPS = 32
C = 640
W = 64
RP = 8
TOK = RP * W
HEADS = C // HEAD_DIM
VROWS = 80
MINE = HEADS // 2
HALF_C = C // 2
QUERIES = 2 * TOK
HALF = 368
BOTH = ("image", "patch")
SCORE_SCALE = HEAD_DIM**-0.5 * 1.4426950408889634
VMEM = pl.BlockSpec(memory_space=pltpu.VMEM)
SMEM = pl.BlockSpec(memory_space=pltpu.SMEM)
ANY = pl.BlockSpec(memory_space=pl.ANY)
HBM = pl.BlockSpec(memory_space=pltpu.HBM)
F32 = jnp.float32
BF16 = jnp.bfloat16


def params(mib):
    return pltpu.CompilerParams(vmem_limit_bytes=mib << 20)


def cost(microseconds):
    return pl.CostEstimate(
        flops=int(microseconds * 1e9), bytes_accessed=int(microseconds * 3e6), transcendentals=0
    )


def near(dims, kind):
    return pltpu.VMEM(dims, kind)


def shape(dims, kind):
    return jax.ShapeDtypeStruct(dims, kind)


def pairs_of(move):
    pairs = []
    for x in range(4):
        for y in range(4):
            for z in range(4):
                for core in range(2):
                    ends = []
                    for a, b, c, d in ((x, y, z, core), move(x, y, z, core)):
                        a, b, c = a % 4, b % 4, c % 4
                        ends.append((a // 2 * 4 + b) * 16 + a % 2 * 8 + c * 2 + d)
                    pairs.append(tuple(ends))
    return pairs


SIBLING = pairs_of(lambda x, y, z, core: (x, y, z, 1 - core))
SIBLINGS = [SIBLING, SIBLING[1:] + SIBLING[:1], SIBLING[2:] + SIBLING[:2]]
Y_UP = pairs_of(lambda x, y, z, core: (x, y + 1, z, core))
Y_DOWN = pairs_of(lambda x, y, z, core: (x, y - 1, z, core))
Z_UP = pairs_of(lambda x, y, z, core: (x, y, z + 1, core))
Z_DOWN = pairs_of(lambda x, y, z, core: (x, y, z - 1, core))
X_LO = pairs_of(lambda x, y, z, core: (x ^ 1, y, z, core))
X_HI = pairs_of(lambda x, y, z, core: (3 - x, y, z, core))


def send(block, pairs):
    return lax.ppermute(block, BOTH, pairs)


def row_live(count, first_row, height):
    rows = lax.broadcasted_iota(jnp.int32, (count, 1), 0) // W + first_row
    return jnp.where(jnp.logical_and(rows >= 0, rows < height), 1.0, 0.0)


def spread(stats_ref, cells, live, live_count):
    mean = jnp.sum(cells * live, axis=0, keepdims=True) / jnp.maximum(live_count, 1.0)
    centred = (cells - mean) * live
    both = jnp.concatenate([mean, jnp.sum(centred * centred, axis=0, keepdims=True)], axis=0)
    for i in range(16):
        stats_ref[i] = both


def stats_kernel(place_ref, image_ref, out_ref):
    first_row, height = place_ref[0], place_ref[1]
    count = (jnp.clip(height - first_row, 0, RP) * W).astype(F32)
    spread(out_ref, image_ref[...].astype(F32), row_live(TOK, first_row, height), count)


def half_kernel(place_ref, own_ref, out_ref, sem):
    start = pl.multiple_of(place_ref[2] * (9 * 80 - HALF), 16)
    copy = pltpu.make_async_copy(own_ref.at[pl.ds(start, HALF), :], out_ref, sem)
    copy.start()
    copy.wait()


GROUPS_OF_SLOTS = ((0, 4, 384), (4, 3, 256), (7, 1, 128))


def activate_kernel(
    place_ref, image_ref, above_ref, below_ref, affine_ref, *outs
):
    first_row, height = place_ref[0], place_ref[1]
    mean, gain, shift = affine_ref[0:1, :], affine_ref[1:2, :], affine_ref[2:3, :]
    channel = lax.broadcasted_iota(jnp.int32, (C, 128), 0)
    order = []
    for first_slot, slots, width in GROUPS_OF_SLOTS:
        wanted = []
        for at in range(0, width, 128):
            lane = lax.broadcasted_iota(jnp.int32, (1, 128), 1) + at
            source = jnp.full((1, 128), -1, jnp.int32)
            for s in range(slots):
                base = place_ref[3 + first_slot + s] * 80 - s * 80
                inside = jnp.logical_and(lane >= s * 80, lane < (s + 1) * 80)
                source = jnp.where(inside, lane + base, source)
            wanted.append(jnp.where(channel == source, 1.0, 0.0).astype(BF16))
        order.append(jnp.concatenate(wanted, axis=1))

    def put(at, count, block, row):
        live = row_live(count, row, height)
        v = (block.astype(F32) * live - mean) * gain + shift
        active = (v / (1.0 + jnp.exp(-v)) * live).astype(BF16)
        for matrix, out in zip(order, outs):
            out[at : at + count, :] = jnp.dot(
                active, matrix, preferred_element_type=F32
            ).astype(BF16)

    put(0, W, above_ref[...], first_row - 1)
    put(W, TOK, image_ref[...], first_row)
    put(W + TOK, W, below_ref[...], first_row + RP)


def weights_kernel(place_ref, wq_ref, wk_ref, wv_ref, wq_t_ref, wk_half_ref, wv_t_ref, turned):
    first_head = pl.ds(pl.multiple_of(place_ref[2] * HALF_C, HALF_C), HALF_C)
    turned[...] = wq_ref[...].T
    wq_t_ref[...] = turned[first_head, :]
    turned[...] = wv_ref[...].T
    wv_t_ref[...] = turned[first_head, :]
    turned[...] = wk_ref[...].T
    wk_half_ref[...] = turned[first_head, :].T


def conv_part(group, place_ref, first_ref, own_ref, mine, theirs, put):
    first_slot, slots, width = GROUPS_OF_SLOTS[group]
    remote = len(mine)
    pad = width - slots * 80

    def from_mine(i, row, rows):
        return mine[i][row : row + rows, :]

    def from_theirs(i, row, rows):
        return theirs[i][row : row + rows, :]

    def run(low, high):
        columns = lax.broadcasted_iota(jnp.int32, (TOK, 1), 0) % W

        def tap_weight(tap):
            pieces = [] if own_ref is None else [own_ref[80 * tap : 80 * tap + 80, :]]
            for i in range(remote):
                if tap <= 3:
                    pieces.append(low(i, 80 * tap, 80))
                elif tap >= 5:
                    pieces.append(high(i, 80 * tap - 352, 80))
                else:
                    pieces += [low(i, 320, 48), high(i, 16, 32)]
            return jnp.concatenate(pieces + [jnp.zeros((pad, C), BF16)], axis=0)

        total = None
        for dx in (0, 1, 2):
            part = None
            for dy in range(3):
                product = jnp.dot(
                    first_ref[dy * W : dy * W + TOK, :],
                    tap_weight(dy * 3 + dx),
                    preferred_element_type=F32,
                )
                part = product if part is None else part + product
            if dx == 0:
                part = jnp.where(columns == 0, 0.0, pltpu.roll(part, 1, 0))
            if dx == 2:
                part = jnp.where(columns == W - 1, 0.0, pltpu.roll(part, TOK - 1, 0))
            total = part if total is None else total + part
        put(total)

    pl.when(place_ref[2] == 0)(lambda: run(from_mine, from_theirs))
    pl.when(place_ref[2] != 0)(lambda: run(from_theirs, from_mine))


def conv_open_kernel(place_ref, first_ref, own_ref, a, b, c, d, e, f, out_ref):
    def put(total):
        out_ref[...] = total

    conv_part(0, place_ref, first_ref, own_ref, (a, b, c), (d, e, f), put)


def conv_more_kernel(place_ref, first_ref, a, b, c, d, e, f, held_ref, out_ref):
    def put(total):
        out_ref[...] = held_ref[...] + total

    conv_part(1, place_ref, first_ref, None, (a, b, c), (d, e, f), put)


def conv_close_kernel(
    place_ref, first_ref, a, theirs_ref, held_ref, image_ref, bias_ref, resid_ref, stats_ref
):
    first_row, height = place_ref[0], place_ref[1]
    live = row_live(TOK, first_row, height)

    def put(total):
        start = image_ref[...].astype(F32) * live
        conv = held_ref[...] + total
        resid_ref[...] = ((start + conv + bias_ref[...]) * live).astype(BF16)

    conv_part(2, place_ref, first_ref, None, (a,), (theirs_ref,), put)
    count = (jnp.clip(height - first_row, 0, RP) * W).astype(F32)
    spread(stats_ref, resid_ref[...].astype(F32), live, count)


def transposed(weight_t, block):
    return lax.dot_general(
        weight_t, block, (((1,), (1,)), ((), ())), preferred_element_type=F32
    ).astype(BF16)


def normalized(place_ref, affine_ref, row, block):
    mean, gain, shift = affine_ref[0:1, :], affine_ref[1:2, :], affine_ref[2:3, :]
    v = (block.astype(F32) - mean) * gain + shift
    return (v * row_live(TOK, row, place_ref[1])).astype(BF16)


def project_pair(place_ref, affine_ref, blocks, wk_ref, wv_ref, keys_ref, values_ref):
    second, ones = [], []
    for n, ref in enumerate(blocks):
        row = place_ref[2 + n]
        second.append(normalized(place_ref, affine_ref, row, ref[...]))
        ones.append(count_row(TOK, row, place_ref[1]))
    second = jnp.concatenate(second, axis=0)
    keys_ref[:, 0:HALF_C] = jnp.dot(second, wk_ref[...], preferred_element_type=F32).astype(BF16)
    keys_ref[:, HALF_C:] = jnp.zeros((QUERIES, 3 * 128 - HALF_C), BF16)
    values_ref[...] = transposed(wv_ref[...], second)
    return jnp.concatenate(ones, axis=1)


def count_row(count, first_row, height):
    tokens = lax.broadcasted_iota(jnp.int32, (VROWS - HEAD_DIM, count), 1)
    lines = lax.broadcasted_iota(jnp.int32, (VROWS - HEAD_DIM, count), 0)
    used = jnp.logical_and(lines == 0, tokens // W + first_row < height)
    return jnp.where(used, 1.0, 0.0).astype(BF16)


def scores_of(keys, query_ref, h):
    return jnp.dot(keys, query_ref[h], preferred_element_type=F32) * SCORE_SCALE


def attend_exactly(place_ref, query_ref, held, acc_ref, top_ref, keys_ref, values_ref):
    parts = QUERIES // 128

    def start(h, _):
        acc_ref[h] = jnp.zeros((VROWS, QUERIES), F32) if held[0] is None else held[0][h]
        return 0

    def step(i, _):
        h, part = i // parts, i % parts
        row = place_ref[2 + part // 4] + part % 4 * 2
        at = pl.ds(pl.multiple_of(part * 128, 128), 128)
        pair = pl.ds(pl.multiple_of(h // 2 * 128, 128), 128)
        shut = row_live(128, row, place_ref[1]) * 1e30 - 1e30
        s = scores_of(keys_ref[at, pair], query_ref, h) + shut
        before = top_ref[h, 0:1, :]
        top = jnp.maximum(before, jnp.max(s, axis=0, keepdims=True))
        head = pl.ds(pl.multiple_of(h * HEAD_DIM, HEAD_DIM), HEAD_DIM)
        value = jnp.concatenate(
            [values_ref[head, at], count_row(128, row, place_ref[1])], axis=0
        )
        weights = jnp.exp2(s - top).astype(BF16)
        update = jnp.dot(value, weights, preferred_element_type=F32)
        acc_ref[h] = acc_ref[h] * jnp.exp2(before - top) + update
        top_ref[h] = jnp.broadcast_to(top, (8, QUERIES))
        return 0

    lax.fori_loop(0, MINE, start, 0)
    lax.fori_loop(0, MINE * parts, step, 0)


def attend_pair(
    place_ref, affine_ref, blocks, wk_ref, wv_ref, query_ref, held, acc_ref, top_ref, scratch
):
    keys_ref, values_ref = scratch
    ones = project_pair(
        place_ref, affine_ref, blocks, wk_ref, wv_ref, keys_ref, values_ref
    )
    far = jnp.zeros((1, QUERIES), F32)
    for h in range(MINE):
        pair = keys_ref[:, h // 2 * 128 : (h // 2 + 1) * 128]
        weights = jnp.exp2(scores_of(pair, query_ref, h) - held[1][h, 0:1, :]).astype(BF16)
        value = jnp.concatenate(
            [values_ref[h * HEAD_DIM : (h + 1) * HEAD_DIM, :], ones], axis=0
        )
        update = jnp.dot(value, weights, preferred_element_type=F32)
        inside = update[HEAD_DIM : HEAD_DIM + 1, :] < 2.0**100
        far = jnp.maximum(far, jnp.where(inside, 0.0, 1.0))
        acc_ref[h] = update if held[0] is None else held[0][h] + update
    top_ref[...] = held[1][...]

    @pl.when(jnp.max(far) > 0.0)
    def _():
        attend_exactly(place_ref, query_ref, held, acc_ref, top_ref, keys_ref, values_ref)


def open_kernel(place_ref, affine_ref, own_ref, other_ref, wq_ref, wk_ref, wv_ref, *refs):
    query_ref, acc_ref, top_ref, first_ref, near_wq_ref, sem, *scratch = refs
    copy = pltpu.make_async_copy(wq_ref, near_wq_ref, sem)
    copy.start()
    blocks = (own_ref, other_ref)
    second = [
        normalized(place_ref, affine_ref, place_ref[2 + n], ref[...])
        for n, ref in enumerate(blocks)
    ]
    copy.wait()
    for n in range(2):
        q = transposed(near_wq_ref[...], second[n])
        span = slice(n * TOK, (n + 1) * TOK)
        zero = jnp.zeros((HEAD_DIM, TOK), BF16)
        for h in range(MINE):
            here, there = h % 2 * HEAD_DIM, (h + 1) % 2 * HEAD_DIM
            query_ref[h, here : here + HEAD_DIM, span] = q[h * HEAD_DIM : (h + 1) * HEAD_DIM]
            query_ref[h, there : there + HEAD_DIM, span] = zero
    opening, shut = [], []
    for n, ref in enumerate(blocks):
        live = row_live(W, place_ref[2 + n], place_ref[1])
        mean, gain, shift = affine_ref[0:1, :], affine_ref[1:2, :], affine_ref[2:3, :]
        v = (ref[0:W, :].astype(F32) - mean) * gain + shift
        opening.append((v * live).astype(BF16))
        shut.append(live * 1e30 - 1e30)
    keys = jnp.dot(jnp.concatenate(opening, axis=0), wk_ref[...], preferred_element_type=F32)
    keys = jnp.concatenate([keys, jnp.zeros((2 * W, 3 * 128 - HALF_C), F32)], axis=1).astype(BF16)
    shut = jnp.concatenate(shut, axis=0)
    for h in range(MINE):
        pair = keys[:, h // 2 * 128 : (h // 2 + 1) * 128]
        top = jnp.max(scores_of(pair, query_ref, h) + shut, axis=0, keepdims=True)
        top = jnp.where(top < -1e29, 0.0, top)
        first_ref[h] = jnp.broadcast_to(top, (8, QUERIES))
    attend_pair(
        place_ref,
        affine_ref,
        blocks,
        wk_ref,
        wv_ref,
        query_ref,
        (None, first_ref),
        acc_ref,
        top_ref,
        scratch,
    )


def attend_kernel(
    place_ref, affine_ref, query_ref, wk_ref, wv_ref, a, b, held_ref, before_ref, *refs
):
    acc_ref, top_ref, *scratch = refs
    held = held_ref, before_ref
    attend_pair(
        place_ref, affine_ref, (a, b), wk_ref, wv_ref, query_ref, held, acc_ref, top_ref, scratch
    )


def close_kernel(
    place_ref, affine_ref, query_ref, wk_ref, wv_ref, a, b, held_ref, before_ref, *refs
):
    mixed_ref, others_ref, acc_ref, top_ref, *scratch = refs
    held = held_ref, before_ref
    attend_pair(
        place_ref, affine_ref, (a, b), wk_ref, wv_ref, query_ref, held, acc_ref, top_ref, scratch
    )
    for h in range(MINE):
        mixed = acc_ref[h, 0:HEAD_DIM, :] / acc_ref[h, HEAD_DIM : HEAD_DIM + 1, :]
        mixed = mixed.astype(BF16)
        for n, ref in enumerate((mixed_ref, others_ref)):
            ref[h * HEAD_DIM : (h + 1) * HEAD_DIM, :] = mixed[:, n * TOK : (n + 1) * TOK]


def finish_kernel(place_ref, mixed_ref, other_ref, resid_ref, wo_ref, bias_ref, out_ref):
    core = place_ref[2]
    update = None
    for at, ref in ((core, mixed_ref), (1 - core, other_ref)):
        rows = pl.ds(pl.multiple_of(at * HALF_C, HALF_C), HALF_C)
        part = lax.dot_general(
            ref[...], wo_ref[rows, :], (((0,), (0,)), ((), ())), preferred_element_type=F32
        )
        update = part if update is None else update + part
    live = row_live(TOK, place_ref[0], place_ref[1])
    out_ref[...] = ((resid_ref[...].astype(F32) + update + bias_ref[...]) * live).astype(BF16)


def exchange(stats):
    return lax.all_to_all(stats, "patch", 0, 0, tiled=False)


def combine_kernel(place_ref, far_ref, gain_ref, shift_ref, out_ref, everyone_ref, sem):
    copy = pltpu.make_async_copy(far_ref, everyone_ref, sem)
    copy.start()
    height = place_ref[1]
    patch = lax.broadcasted_iota(jnp.int32, (16, 1), 0)
    counts = (jnp.clip(height - RP * patch, 0, RP) * W).astype(F32)
    entries = (height * W * (C // GROUPS)).astype(F32)
    channel = lax.broadcasted_iota(jnp.int32, (C, 128), 0)
    group = lax.broadcasted_iota(jnp.int32, (C, 128), 1)
    member = jnp.where(channel // (C // GROUPS) == group, 1.0, 0.0)

    def over_group(line):
        lines = jnp.broadcast_to(line, (8, C))
        return lax.dot_general(
            lines,
            member,
            (((1,), (0,)), ((), ())),
            precision=lax.Precision.HIGHEST,
            preferred_element_type=F32,
        )

    def widened(groups):
        return lax.dot_general(
            groups,
            member,
            (((1,), (1,)), ((), ())),
            precision=lax.Precision.HIGHEST,
            preferred_element_type=F32,
        )

    copy.wait()
    means, squares = everyone_ref[:, 0, :], everyone_ref[:, 1, :]
    mean = widened(over_group(jnp.sum(means * counts, axis=0, keepdims=True)) / entries)
    apart = means - mean[0:1, :]
    spread_sum = jnp.sum(squares + counts * apart * apart, axis=0, keepdims=True)
    scale = widened(lax.rsqrt(over_group(spread_sum) / entries + 1e-05))
    out_ref[0:1, :] = mean[0:1, :]
    out_ref[1:2, :] = scale[0:1, :] * gain_ref[...]
    out_ref[2:3, :] = shift_ref[...]


def combine(place, everyone, gain, shift):
    return pl.pallas_call(
        combine_kernel,
        in_specs=[SMEM, ANY] + [VMEM] * 2,
        out_specs=VMEM,
        out_shape=near((3, C), F32),
        scratch_shapes=[pltpu.VMEM((16, 2, C), F32), pltpu.SemaphoreType.DMA],
        compiler_params=params(16),
    )(place, everyone, gain[None, :], shift[None, :])


def per_device(
    images,
    heights,
    opening_scale_vector,
    opening_offset_vector,
    conv_weight,
    kernel_offset_vector,
    closing_scale_vector,
    closing_offset_vector,
    query_weight,
    key_weight,
    value_weight,
    out_weight,
    out_bias,
):
    image = images[0].reshape(TOK, C)
    height = heights[0]
    at_image = lax.axis_index("image")
    at_patch = lax.axis_index("patch")
    core = at_patch % 2
    first_row = at_patch * RP
    x_hi, y = at_image // 4, at_image % 4
    x_lo, z = at_patch // 8, at_patch // 2 % 4
    a_at = lambda by: x_hi * 4 + (y + by) % 4
    b_at = lambda by: (1 - x_hi) * 4 + (y + by) % 4
    place = jnp.stack(
        [first_row, height, core, at_image]
        + [a_at(3), a_at(1), b_at(0), a_at(2), b_at(3), b_at(1), b_at(2)]
    )

    own = conv_weight.reshape(9 * 80, C)
    half = pl.pallas_call(
        half_kernel,
        in_specs=[SMEM, HBM],
        out_specs=VMEM,
        out_shape=near((HALF, C), BF16),
        scratch_shapes=[pltpu.SemaphoreType.DMA],
        compiler_params=params(8),
    )(place, own)
    a_up = send(half, Y_UP)
    a_down = send(half, Y_DOWN)
    b_own = send(half, X_HI)

    stats = pl.pallas_call(
        stats_kernel,
        in_specs=[SMEM, VMEM],
        out_specs=VMEM,
        out_shape=shape((16, 2, C), F32),
        compiler_params=params(16),
    )(place, image)
    everyone = exchange(stats)
    a_up, a_down, b_own, everyone, bottom, top_row = lax.optimization_barrier(
        (a_up, a_down, b_own, everyone, image[TOK - W :], image[:W])
    )
    a_far = send(a_up, Y_UP)
    b_up = send(a_up, X_HI)
    b_down = send(b_own, Y_DOWN)
    up_pairs = [(g * 16 + i, g * 16 + i + 1) for g in range(8) for i in range(15)]
    above = send(bottom, up_pairs)
    below = send(top_row, [(b, a) for a, b in up_pairs])
    affine = combine(place, everyone, opening_scale_vector, opening_offset_vector)

    widths = [width for _, _, width in GROUPS_OF_SLOTS]
    first = pl.pallas_call(
        activate_kernel,
        in_specs=[SMEM] + [VMEM] * 4,
        out_specs=[VMEM] * 3,
        out_shape=[near((TOK + 2 * W, width), BF16) for width in widths],
        compiler_params=params(20),
        cost_estimate=cost(3),
    )(place, image, above, below, affine)
    widths = [width for _, _, width in GROUPS_OF_SLOTS]
    first = pl.pallas_call(
        activate_kernel,
        in_specs=[SMEM] + [VMEM] * 4,
        out_specs=[VMEM] * 3,
        out_shape=[near((TOK + 2 * W, width), BF16) for width in widths],
        compiler_params=params(20),
        cost_estimate=cost(3),
    )(place, image, above, below, affine)
    theirs_1 = [send(b, p) for b, p in zip((a_up, a_down, b_own), SIBLINGS)]
    mine_1, first = lax.optimization_barrier(([a_up, a_down, b_own], first))
    theirs_1 = [send(b, p) for b, p in zip(mine_1, SIBLINGS)]
    mine_2, theirs_1, first = lax.optimization_barrier(([a_far, b_up, b_down], theirs_1, first))
    b_far = send(mine_2[0], X_HI)
    theirs_2 = [send(b, p) for b, p in zip(mine_2, SIBLINGS)]
    conv = pl.pallas_call(
        conv_open_kernel,
        in_specs=[SMEM] + [VMEM] * 8,
        out_specs=VMEM,
        out_shape=near((TOK, C), F32),
        compiler_params=params(20),
        cost_estimate=cost(5),
    )(place, first[0], own, a_up, a_down, b_own, *theirs_1)
    conv, *qkv = lax.optimization_barrier((conv, query_weight, key_weight, value_weight))
    wq_t, wk, wv_t = pl.pallas_call(
        weights_kernel,
        in_specs=[SMEM] + [VMEM] * 3,
        out_specs=[VMEM] * 3,
        out_shape=[near(dims, BF16) for dims in ((HALF_C, C), (C, HALF_C), (HALF_C, C))],
        scratch_shapes=[pltpu.VMEM((C, C), BF16)],
        compiler_params=params(20),
        cost_estimate=cost(3),
    )(place, *qkv)
    b_far, theirs_2, conv, wq_t, wk, wv_t = lax.optimization_barrier(
        (b_far, theirs_2, conv, wq_t, wk, wv_t)
    )
    conv = pl.pallas_call(
        conv_more_kernel,
        in_specs=[SMEM] + [VMEM] * 8,
        out_specs=VMEM,
        out_shape=near((TOK, C), F32),
        input_output_aliases={8: 0},
        compiler_params=params(20),
        cost_estimate=cost(4),
    )(place, first[1], *mine_2, *theirs_2, conv)
    theirs_3 = send(b_far, SIBLING)
    resid, stats = pl.pallas_call(
        conv_close_kernel,
        in_specs=[SMEM] + [VMEM] * 6,
        out_specs=[VMEM, VMEM],
        out_shape=[near((TOK, C), BF16), shape((16, 2, C), F32)],
        compiler_params=params(20),
    )(place, first[2], b_far, theirs_3, conv, image, kernel_offset_vector[None, :])

    everyone = exchange(stats)
    mine_0, everyone = lax.optimization_barrier((resid, everyone))
    other_0 = send(mine_0, SIBLING)
    c_up = send(mine_0, Z_UP)
    c_down = send(mine_0, Z_DOWN)
    d_own = send(mine_0, X_LO)
    affine = combine(place, everyone, closing_scale_vector, closing_offset_vector)
    c_row = lambda by, at: (x_lo * 8 + (z + by) % 4 * 2 + at) * RP
    d_row = lambda by, at: ((1 - x_lo) * 8 + (z + by) % 4 * 2 + at) * RP
    rows_of = lambda at: [
        [c_row(0, at)],
        [c_row(3, at), c_row(1, at), d_row(0, at)],
        [c_row(2, at), d_row(3, at), d_row(1, at)],
        [d_row(2, at)],
    ]
    mine, theirs = rows_of(core), rows_of(1 - core)

    def rows_place(rows):
        return jnp.stack([first_row, height] + rows)

    acc_shape = (MINE, VROWS, QUERIES)

    top_shape = (MINE, 8, QUERIES)
    pair_scratch = [pltpu.VMEM((QUERIES, 3 * 128), BF16), pltpu.VMEM((HALF_C, QUERIES), BF16)]

    def attend(blocks, rows, state):
        return pl.pallas_call(
            attend_kernel,
            in_specs=[SMEM] + [VMEM] * 8,
            out_specs=[VMEM] * 2,
            out_shape=[near(acc_shape, F32), near(top_shape, F32)],
            scratch_shapes=pair_scratch,
            compiler_params=params(24),
        )(rows_place(rows), affine, query, wk, wv_t, *blocks, *state)

    def held_until(blocks, state):
        return lax.optimization_barrier((blocks, state))

    query, *state = pl.pallas_call(
        open_kernel,
        in_specs=[SMEM] + [VMEM] * 3 + [ANY] + [VMEM] * 2,
        out_specs=[VMEM] * 3,
        out_shape=[
            near((MINE, 2 * HEAD_DIM, QUERIES), BF16),
            near(acc_shape, F32),
            near(top_shape, F32),
        ],
        scratch_shapes=[
            pltpu.VMEM(top_shape, F32),
            pltpu.VMEM((HALF_C, C), BF16),
            pltpu.SemaphoreType.DMA,
        ]
        + pair_scratch,
        compiler_params=params(24),
    )(rows_place(mine[0] + theirs[0]), affine, resid, other_0, wq_t, wk, wv_t)

    mine_1, state = held_until([c_up, c_down, d_own], state)
    c_far = send(mine_1[0], Z_UP)
    d_up = send(mine_1[0], X_LO)
    d_down = send(mine_1[2], Z_DOWN)
    other_1 = [send(mine_1[0], SIBLING)]
    state = attend(mine_1[:2], mine[1][:2], state)
    (late, other_1), state = held_until((mine_1[1:], other_1), state)
    other_1 += [send(block, pairs) for block, pairs in zip(late, SIBLINGS)]
    state = attend([late[1], other_1[0]], mine[1][2:] + theirs[1][:1], state)
    mine_2, state = held_until([c_far, d_up, d_down], state)
    last = send(mine_2[0], X_LO)
    other_2 = [send(block, pairs) for block, pairs in zip(mine_2, SIBLINGS)]
    state = attend(other_1[1:], theirs[1][1:], state)
    state = attend(mine_2[:2], mine[2][:2], state)
    state = attend([mine_2[2], other_2[0]], mine[2][2:] + theirs[2][:1], state)
    (last, other_2), state = held_until((last, other_2), state)
    other_3 = send(last, SIBLING)
    state = attend(other_2[1:], theirs[2][1:], state)
    other_3, state = held_until(other_3, state)

    mixed, others = pl.pallas_call(
        close_kernel,
        in_specs=[SMEM] + [VMEM] * 8,
        out_specs=[VMEM] * 2,
        out_shape=[near((HALF_C, TOK), BF16)] * 2,
        scratch_shapes=[pltpu.VMEM(acc_shape, F32), pltpu.VMEM(top_shape, F32)] + pair_scratch,
        compiler_params=params(24),
    )(rows_place(mine[3] + theirs[3]), affine, query, wk, wv_t, last, other_3, *state)
    other = send(others, SIBLING)
    out = pl.pallas_call(
        finish_kernel,
        in_specs=[SMEM] + [VMEM] * 5,
        out_specs=VMEM,
        out_shape=shape((TOK, C), BF16),
        compiler_params=params(20),
    )(place, mixed, other, resid, out_weight, out_bias[None, :])
    return out.reshape(1, RP, W, C)


def solution(mesh):
    in_specs = (
        P("image", "patch", None, None),
        P("image"),
        P(),
        P(),
        P(None, None, "image", None),
        P(),
        P(),
        P(),
        P(),
        P(),
        P(),
        P(),
        P(),
    )
    out_specs = P("image", "patch", None, None)
    return jax.shard_map(
        per_device, mesh=mesh, in_specs=in_specs, out_specs=out_specs, check_vma=False
    )
```

```python
import functools

import jax
import jax.numpy as jnp
from jax import lax
from jax.experimental import pallas as pl
from jax.experimental.pallas import tpu as pltpu
from jax.sharding import PartitionSpec as P

HEAD_DIM = 64
GROUPS = 32
C = 640
W = 64
RP = 8
TOK = RP * W
HEADS = C // HEAD_DIM
VROWS = 80
MINE = HEADS // 2
HALF_C = C // 2
QUERIES = 2 * TOK
HALF = 368
BOTH = ("image", "patch")
SCORE_SCALE = HEAD_DIM**-0.5 * 1.4426950408889634
VMEM = pl.BlockSpec(memory_space=pltpu.VMEM)
SMEM = pl.BlockSpec(memory_space=pltpu.SMEM)
ANY = pl.BlockSpec(memory_space=pl.ANY)
HBM = pl.BlockSpec(memory_space=pltpu.HBM)
F32 = jnp.float32
BF16 = jnp.bfloat16


def params(mib):
    return pltpu.CompilerParams(vmem_limit_bytes=mib << 20)


def cost(microseconds):
    return pl.CostEstimate(
        flops=int(microseconds * 1e9), bytes_accessed=int(microseconds * 3e6), transcendentals=0
    )


def near(dims, kind):
    return pltpu.VMEM(dims, kind)


def shape(dims, kind):
    return jax.ShapeDtypeStruct(dims, kind)


def pairs_of(move):
    pairs = []
    for x in range(4):
        for y in range(4):
            for z in range(4):
                for core in range(2):
                    ends = []
                    for a, b, c, d in ((x, y, z, core), move(x, y, z, core)):
                        a, b, c = a % 4, b % 4, c % 4
                        ends.append((a // 2 * 4 + b) * 16 + a % 2 * 8 + c * 2 + d)
                    pairs.append(tuple(ends))
    return pairs


SIBLING = pairs_of(lambda x, y, z, core: (x, y, z, 1 - core))
SIBLINGS = [SIBLING, SIBLING[1:] + SIBLING[:1], SIBLING[2:] + SIBLING[:2]]
Y_UP = pairs_of(lambda x, y, z, core: (x, y + 1, z, core))
Y_DOWN = pairs_of(lambda x, y, z, core: (x, y - 1, z, core))
Z_UP = pairs_of(lambda x, y, z, core: (x, y, z + 1, core))
Z_DOWN = pairs_of(lambda x, y, z, core: (x, y, z - 1, core))
X_LO = pairs_of(lambda x, y, z, core: (x ^ 1, y, z, core))
X_HI = pairs_of(lambda x, y, z, core: (3 - x, y, z, core))


def send(block, pairs):
    return lax.ppermute(block, BOTH, pairs)


def row_live(count, first_row, height):
    rows = lax.broadcasted_iota(jnp.int32, (count, 1), 0) // W + first_row
    return jnp.where(jnp.logical_and(rows >= 0, rows < height), 1.0, 0.0)


def spread(stats_ref, cells, live, live_count):
    mean = jnp.sum(cells * live, axis=0, keepdims=True) / jnp.maximum(live_count, 1.0)
    centred = (cells - mean) * live
    both = jnp.concatenate([mean, jnp.sum(centred * centred, axis=0, keepdims=True)], axis=0)
    for i in range(16):
        stats_ref[i] = both


def stats_kernel(place_ref, image_ref, out_ref):
    first_row, height = place_ref[0], place_ref[1]
    count = (jnp.clip(height - first_row, 0, RP) * W).astype(F32)
    spread(out_ref, image_ref[...].astype(F32), row_live(TOK, first_row, height), count)


def half_kernel(place_ref, own_ref, out_ref, sem):
    start = pl.multiple_of(place_ref[2] * (9 * 80 - HALF), 16)
    copy = pltpu.make_async_copy(own_ref.at[pl.ds(start, HALF), :], out_ref, sem)
    copy.start()
    copy.wait()


GROUPS_OF_SLOTS = ((0, 4, 384), (4, 3, 256), (7, 1, 128))


def activate_kernel(
    place_ref, image_ref, above_ref, below_ref, affine_ref, *outs
):
    first_row, height = place_ref[0], place_ref[1]
    mean, gain, shift = affine_ref[0:1, :], affine_ref[1:2, :], affine_ref[2:3, :]
    channel = lax.broadcasted_iota(jnp.int32, (C, 128), 0)
    order = []
    for first_slot, slots, width in GROUPS_OF_SLOTS:
        wanted = []
        for at in range(0, width, 128):
            lane = lax.broadcasted_iota(jnp.int32, (1, 128), 1) + at
            source = jnp.full((1, 128), -1, jnp.int32)
            for s in range(slots):
                base = place_ref[3 + first_slot + s] * 80 - s * 80
                inside = jnp.logical_and(lane >= s * 80, lane < (s + 1) * 80)
                source = jnp.where(inside, lane + base, source)
            wanted.append(jnp.where(channel == source, 1.0, 0.0).astype(BF16))
        order.append(jnp.concatenate(wanted, axis=1))

    def put(at, count, block, row):
        live = row_live(count, row, height)
        v = (block.astype(F32) * live - mean) * gain + shift
        active = (v / (1.0 + jnp.exp(-v)) * live).astype(BF16)
        for matrix, out in zip(order, outs):
            out[at : at + count, :] = jnp.dot(
                active, matrix, preferred_element_type=F32
            ).astype(BF16)

    put(0, W, above_ref[...], first_row - 1)
    put(W, TOK, image_ref[...], first_row)
    put(W + TOK, W, below_ref[...], first_row + RP)


def weights_kernel(place_ref, wq_ref, wk_ref, wv_ref, wq_t_ref, wk_half_ref, wv_t_ref, turned):
    first_head = pl.ds(pl.multiple_of(place_ref[2] * HALF_C, HALF_C), HALF_C)
    turned[...] = wq_ref[...].T
    wq_t_ref[...] = turned[first_head, :]
    turned[...] = wv_ref[...].T
    wv_t_ref[...] = turned[first_head, :]
    turned[...] = wk_ref[...].T
    wk_half_ref[...] = turned[first_head, :].T


def conv_part(group, place_ref, first_ref, own_ref, mine, theirs, put):
    first_slot, slots, width = GROUPS_OF_SLOTS[group]
    remote = len(mine)
    pad = width - slots * 80

    def from_mine(i, row, rows):
        return mine[i][row : row + rows, :]

    def from_theirs(i, row, rows):
        return theirs[i][row : row + rows, :]

    def run(low, high):
        columns = lax.broadcasted_iota(jnp.int32, (TOK, 1), 0) % W

        def tap_weight(tap):
            pieces = [] if own_ref is None else [own_ref[80 * tap : 80 * tap + 80, :]]
            for i in range(remote):
                if tap <= 3:
                    pieces.append(low(i, 80 * tap, 80))
                elif tap >= 5:
                    pieces.append(high(i, 80 * tap - 352, 80))
                else:
                    pieces += [low(i, 320, 48), high(i, 16, 32)]
            return jnp.concatenate(pieces + [jnp.zeros((pad, C), BF16)], axis=0)

        total = None
        for dx in (0, 1, 2):
            part = None
            for dy in range(3):
                product = jnp.dot(
                    first_ref[dy * W : dy * W + TOK, :],
                    tap_weight(dy * 3 + dx),
                    preferred_element_type=F32,
                )
                part = product if part is None else part + product
            if dx == 0:
                part = jnp.where(columns == 0, 0.0, pltpu.roll(part, 1, 0))
            if dx == 2:
                part = jnp.where(columns == W - 1, 0.0, pltpu.roll(part, TOK - 1, 0))
            total = part if total is None else total + part
        put(total)

    pl.when(place_ref[2] == 0)(lambda: run(from_mine, from_theirs))
    pl.when(place_ref[2] != 0)(lambda: run(from_theirs, from_mine))


def conv_open_kernel(place_ref, first_ref, own_ref, a, b, c, d, e, f, out_ref):
    def put(total):
        out_ref[...] = total

    conv_part(0, place_ref, first_ref, own_ref, (a, b, c), (d, e, f), put)


def conv_more_kernel(place_ref, first_ref, a, b, c, d, e, f, held_ref, out_ref):
    def put(total):
        out_ref[...] = held_ref[...] + total

    conv_part(1, place_ref, first_ref, None, (a, b, c), (d, e, f), put)


def conv_close_kernel(
    place_ref, first_ref, a, theirs_ref, held_ref, image_ref, bias_ref, resid_ref, stats_ref
):
    first_row, height = place_ref[0], place_ref[1]
    live = row_live(TOK, first_row, height)

    def put(total):
        start = image_ref[...].astype(F32) * live
        conv = held_ref[...] + total
        resid_ref[...] = ((start + conv + bias_ref[...]) * live).astype(BF16)

    conv_part(2, place_ref, first_ref, None, (a,), (theirs_ref,), put)
    count = (jnp.clip(height - first_row, 0, RP) * W).astype(F32)
    spread(stats_ref, resid_ref[...].astype(F32), live, count)


def transposed(weight_t, block):
    return lax.dot_general(
        weight_t, block, (((1,), (1,)), ((), ())), preferred_element_type=F32
    ).astype(BF16)


def normalized(place_ref, affine_ref, row, block):
    mean, gain, shift = affine_ref[0:1, :], affine_ref[1:2, :], affine_ref[2:3, :]
    v = (block.astype(F32) - mean) * gain + shift
    return (v * row_live(TOK, row, place_ref[1])).astype(BF16)


def project_pair(place_ref, affine_ref, blocks, wk_ref, wv_ref, keys_ref, values_ref):
    second, ones = [], []
    for n, ref in enumerate(blocks):
        row = place_ref[2 + n]
        second.append(normalized(place_ref, affine_ref, row, ref[...]))
        ones.append(count_row(TOK, row, place_ref[1]))
    second = jnp.concatenate(second, axis=0)
    keys_ref[:, 0:HALF_C] = jnp.dot(second, wk_ref[...], preferred_element_type=F32).astype(BF16)
    keys_ref[:, HALF_C:] = jnp.zeros((QUERIES, 3 * 128 - HALF_C), BF16)
    values_ref[...] = transposed(wv_ref[...], second)
    return jnp.concatenate(ones, axis=1)


def count_row(count, first_row, height):
    tokens = lax.broadcasted_iota(jnp.int32, (VROWS - HEAD_DIM, count), 1)
    lines = lax.broadcasted_iota(jnp.int32, (VROWS - HEAD_DIM, count), 0)
    used = jnp.logical_and(lines == 0, tokens // W + first_row < height)
    return jnp.where(used, 1.0, 0.0).astype(BF16)


def scores_of(keys, query_ref, h):
    return jnp.dot(keys, query_ref[h], preferred_element_type=F32) * SCORE_SCALE


def attend_exactly(place_ref, query_ref, held, acc_ref, top_ref, keys_ref, values_ref):
    parts = QUERIES // 128

    def start(h, _):
        acc_ref[h] = jnp.zeros((VROWS, QUERIES), F32) if held[0] is None else held[0][h]
        return 0

    def step(i, _):
        h, part = i // parts, i % parts
        row = place_ref[2 + part // 4] + part % 4 * 2
        at = pl.ds(pl.multiple_of(part * 128, 128), 128)
        pair = pl.ds(pl.multiple_of(h // 2 * 128, 128), 128)
        shut = row_live(128, row, place_ref[1]) * 1e30 - 1e30
        s = scores_of(keys_ref[at, pair], query_ref, h) + shut
        before = top_ref[h, 0:1, :]
        top = jnp.maximum(before, jnp.max(s, axis=0, keepdims=True))
        head = pl.ds(pl.multiple_of(h * HEAD_DIM, HEAD_DIM), HEAD_DIM)
        value = jnp.concatenate(
            [values_ref[head, at], count_row(128, row, place_ref[1])], axis=0
        )
        weights = jnp.exp2(s - top).astype(BF16)
        update = jnp.dot(value, weights, preferred_element_type=F32)
        acc_ref[h] = acc_ref[h] * jnp.exp2(before - top) + update
        top_ref[h] = jnp.broadcast_to(top, (8, QUERIES))
        return 0

    lax.fori_loop(0, MINE, start, 0)
    lax.fori_loop(0, MINE * parts, step, 0)


def attend_pair(
    place_ref, affine_ref, blocks, wk_ref, wv_ref, query_ref, held, acc_ref, top_ref, scratch
):
    keys_ref, values_ref = scratch
    ones = project_pair(
        place_ref, affine_ref, blocks, wk_ref, wv_ref, keys_ref, values_ref
    )
    far = jnp.zeros((1, QUERIES), F32)
    for h in range(MINE):
        pair = keys_ref[:, h // 2 * 128 : (h // 2 + 1) * 128]
        weights = jnp.exp2(scores_of(pair, query_ref, h) - held[1][h, 0:1, :]).astype(BF16)
        value = jnp.concatenate(
            [values_ref[h * HEAD_DIM : (h + 1) * HEAD_DIM, :], ones], axis=0
        )
        update = jnp.dot(value, weights, preferred_element_type=F32)
        inside = update[HEAD_DIM : HEAD_DIM + 1, :] < 2.0**100
        far = jnp.maximum(far, jnp.where(inside, 0.0, 1.0))
        acc_ref[h] = update if held[0] is None else held[0][h] + update
    top_ref[...] = held[1][...]

    @pl.when(jnp.max(far) > 0.0)
    def _():
        attend_exactly(place_ref, query_ref, held, acc_ref, top_ref, keys_ref, values_ref)


def open_kernel(place_ref, affine_ref, own_ref, other_ref, wq_ref, wk_ref, wv_ref, *refs):
    query_ref, acc_ref, top_ref, first_ref, near_wq_ref, sem, *scratch = refs
    copy = pltpu.make_async_copy(wq_ref, near_wq_ref, sem)
    copy.start()
    blocks = (own_ref, other_ref)
    second = [
        normalized(place_ref, affine_ref, place_ref[2 + n], ref[...])
        for n, ref in enumerate(blocks)
    ]
    copy.wait()
    for n in range(2):
        q = transposed(near_wq_ref[...], second[n])
        span = slice(n * TOK, (n + 1) * TOK)
        zero = jnp.zeros((HEAD_DIM, TOK), BF16)
        for h in range(MINE):
            here, there = h % 2 * HEAD_DIM, (h + 1) % 2 * HEAD_DIM
            query_ref[h, here : here + HEAD_DIM, span] = q[h * HEAD_DIM : (h + 1) * HEAD_DIM]
            query_ref[h, there : there + HEAD_DIM, span] = zero
    opening, shut = [], []
    for n, ref in enumerate(blocks):
        live = row_live(W, place_ref[2 + n], place_ref[1])
        mean, gain, shift = affine_ref[0:1, :], affine_ref[1:2, :], affine_ref[2:3, :]
        v = (ref[0:W, :].astype(F32) - mean) * gain + shift
        opening.append((v * live).astype(BF16))
        shut.append(live * 1e30 - 1e30)
    keys = jnp.dot(jnp.concatenate(opening, axis=0), wk_ref[...], preferred_element_type=F32)
    keys = jnp.concatenate([keys, jnp.zeros((2 * W, 3 * 128 - HALF_C), F32)], axis=1).astype(BF16)
    shut = jnp.concatenate(shut, axis=0)
    for h in range(MINE):
        pair = keys[:, h // 2 * 128 : (h // 2 + 1) * 128]
        top = jnp.max(scores_of(pair, query_ref, h) + shut, axis=0, keepdims=True)
        top = jnp.where(top < -1e29, 0.0, top)
        first_ref[h] = jnp.broadcast_to(top, (8, QUERIES))
    attend_pair(
        place_ref,
        affine_ref,
        blocks,
        wk_ref,
        wv_ref,
        query_ref,
        (None, first_ref),
        acc_ref,
        top_ref,
        scratch,
    )


def attend_kernel(
    place_ref, affine_ref, query_ref, wk_ref, wv_ref, a, b, held_ref, before_ref, *refs
):
    acc_ref, top_ref, *scratch = refs
    held = held_ref, before_ref
    attend_pair(
        place_ref, affine_ref, (a, b), wk_ref, wv_ref, query_ref, held, acc_ref, top_ref, scratch
    )


def close_kernel(
    place_ref, affine_ref, query_ref, wk_ref, wv_ref, a, b, held_ref, before_ref, *refs
):
    mixed_ref, others_ref, acc_ref, top_ref, *scratch = refs
    held = held_ref, before_ref
    attend_pair(
        place_ref, affine_ref, (a, b), wk_ref, wv_ref, query_ref, held, acc_ref, top_ref, scratch
    )
    for h in range(MINE):
        mixed = acc_ref[h, 0:HEAD_DIM, :] / acc_ref[h, HEAD_DIM : HEAD_DIM + 1, :]
        mixed = mixed.astype(BF16)
        for n, ref in enumerate((mixed_ref, others_ref)):
            ref[h * HEAD_DIM : (h + 1) * HEAD_DIM, :] = mixed[:, n * TOK : (n + 1) * TOK]


def finish_kernel(place_ref, mixed_ref, other_ref, resid_ref, wo_ref, bias_ref, out_ref):
    core = place_ref[2]
    update = None
    for at, ref in ((core, mixed_ref), (1 - core, other_ref)):
        rows = pl.ds(pl.multiple_of(at * HALF_C, HALF_C), HALF_C)
        part = lax.dot_general(
            ref[...], wo_ref[rows, :], (((0,), (0,)), ((), ())), preferred_element_type=F32
        )
        update = part if update is None else update + part
    live = row_live(TOK, place_ref[0], place_ref[1])
    out_ref[...] = ((resid_ref[...].astype(F32) + update + bias_ref[...]) * live).astype(BF16)


def exchange(stats):
    return lax.all_to_all(stats, "patch", 0, 0, tiled=False)


def combine_kernel(place_ref, far_ref, gain_ref, shift_ref, out_ref, everyone_ref, sem):
    copy = pltpu.make_async_copy(far_ref, everyone_ref, sem)
    copy.start()
    height = place_ref[1]
    patch = lax.broadcasted_iota(jnp.int32, (16, 1), 0)
    counts = (jnp.clip(height - RP * patch, 0, RP) * W).astype(F32)
    entries = (height * W * (C // GROUPS)).astype(F32)
    channel = lax.broadcasted_iota(jnp.int32, (C, 128), 0)
    group = lax.broadcasted_iota(jnp.int32, (C, 128), 1)
    member = jnp.where(channel // (C // GROUPS) == group, 1.0, 0.0)

    def over_group(line):
        lines = jnp.broadcast_to(line, (8, C))
        return lax.dot_general(
            lines,
            member,
            (((1,), (0,)), ((), ())),
            precision=lax.Precision.HIGHEST,
            preferred_element_type=F32,
        )

    def widened(groups):
        return lax.dot_general(
            groups,
            member,
            (((1,), (1,)), ((), ())),
            precision=lax.Precision.HIGHEST,
            preferred_element_type=F32,
        )

    copy.wait()
    means, squares = everyone_ref[:, 0, :], everyone_ref[:, 1, :]
    mean = widened(over_group(jnp.sum(means * counts, axis=0, keepdims=True)) / entries)
    apart = means - mean[0:1, :]
    spread_sum = jnp.sum(squares + counts * apart * apart, axis=0, keepdims=True)
    scale = widened(lax.rsqrt(over_group(spread_sum) / entries + 1e-05))
    out_ref[0:1, :] = mean[0:1, :]
    out_ref[1:2, :] = scale[0:1, :] * gain_ref[...]
    out_ref[2:3, :] = shift_ref[...]


def combine(place, everyone, gain, shift):
    return pl.pallas_call(
        combine_kernel,
        in_specs=[SMEM, ANY] + [VMEM] * 2,
        out_specs=VMEM,
        out_shape=near((3, C), F32),
        scratch_shapes=[pltpu.VMEM((16, 2, C), F32), pltpu.SemaphoreType.DMA],
        compiler_params=params(16),
    )(place, everyone, gain[None, :], shift[None, :])


def per_device(
    images,
    heights,
    opening_scale_vector,
    opening_offset_vector,
    conv_weight,
    kernel_offset_vector,
    closing_scale_vector,
    closing_offset_vector,
    query_weight,
    key_weight,
    value_weight,
    out_weight,
    out_bias,
):
    image = images[0].reshape(TOK, C)
    height = heights[0]
    at_image = lax.axis_index("image")
    at_patch = lax.axis_index("patch")
    core = at_patch % 2
    first_row = at_patch * RP
    x_hi, y = at_image // 4, at_image % 4
    x_lo, z = at_patch // 8, at_patch // 2 % 4
    a_at = lambda by: x_hi * 4 + (y + by) % 4
    b_at = lambda by: (1 - x_hi) * 4 + (y + by) % 4
    place = jnp.stack(
        [first_row, height, core, at_image]
        + [a_at(3), a_at(1), b_at(0), a_at(2), b_at(3), b_at(1), b_at(2)]
    )

    own = conv_weight.reshape(9 * 80, C)
    half = pl.pallas_call(
        half_kernel,
        in_specs=[SMEM, HBM],
        out_specs=VMEM,
        out_shape=near((HALF, C), BF16),
        scratch_shapes=[pltpu.SemaphoreType.DMA],
        compiler_params=params(8),
    )(place, own)
    a_up = send(half, Y_UP)
    a_down = send(half, Y_DOWN)
    b_own = send(half, X_HI)

    stats = pl.pallas_call(
        stats_kernel,
        in_specs=[SMEM, VMEM],
        out_specs=VMEM,
        out_shape=shape((16, 2, C), F32),
        compiler_params=params(16),
    )(place, image)
    everyone = exchange(stats)
    a_up, a_down, b_own, everyone, bottom, top_row = lax.optimization_barrier(
        (a_up, a_down, b_own, everyone, image[TOK - W :], image[:W])
    )
    b_up = send(a_up, X_HI)
    a_far = send(a_up, Y_UP)
    b_down = send(b_own, Y_DOWN)
    up_pairs = [(g * 16 + i, g * 16 + i + 1) for g in range(8) for i in range(15)]
    above = send(bottom, up_pairs)
    below = send(top_row, [(b, a) for a, b in up_pairs])
    affine = combine(place, everyone, opening_scale_vector, opening_offset_vector)

    widths = [width for _, _, width in GROUPS_OF_SLOTS]
    first = pl.pallas_call(
        activate_kernel,
        in_specs=[SMEM] + [VMEM] * 4,
        out_specs=[VMEM] * 3,
        out_shape=[near((TOK + 2 * W, width), BF16) for width in widths],
        compiler_params=params(20),
        cost_estimate=cost(3),
    )(place, image, above, below, affine)
    widths = [width for _, _, width in GROUPS_OF_SLOTS]
    first = pl.pallas_call(
        activate_kernel,
        in_specs=[SMEM] + [VMEM] * 4,
        out_specs=[VMEM] * 3,
        out_shape=[near((TOK + 2 * W, width), BF16) for width in widths],
        compiler_params=params(20),
        cost_estimate=cost(3),
    )(place, image, above, below, affine)
    theirs_1 = [send(b, p) for b, p in zip((a_up, a_down, b_own), SIBLINGS)]
    mine_1, first = lax.optimization_barrier(([a_up, a_down, b_own], first))
    theirs_1 = [send(b, p) for b, p in zip(mine_1, SIBLINGS)]
    b_up, first = lax.optimization_barrier((b_up, first))
    b_far = send(b_up, Y_UP[1:] + Y_UP[:1])
    mine_2, theirs_1, first = lax.optimization_barrier(([a_far, b_up, b_down], theirs_1, first))
    theirs_2 = [send(b, p) for b, p in zip(mine_2, SIBLINGS)]
    conv = pl.pallas_call(
        conv_open_kernel,
        in_specs=[SMEM] + [VMEM] * 8,
        out_specs=VMEM,
        out_shape=near((TOK, C), F32),
        compiler_params=params(20),
        cost_estimate=cost(5),
    )(place, first[0], own, a_up, a_down, b_own, *theirs_1)
    conv, *qkv = lax.optimization_barrier((conv, query_weight, key_weight, value_weight))
    wq_t, wk, wv_t = pl.pallas_call(
        weights_kernel,
        in_specs=[SMEM] + [VMEM] * 3,
        out_specs=[VMEM] * 3,
        out_shape=[near(dims, BF16) for dims in ((HALF_C, C), (C, HALF_C), (HALF_C, C))],
        scratch_shapes=[pltpu.VMEM((C, C), BF16)],
        compiler_params=params(20),
        cost_estimate=cost(3),
    )(place, *qkv)
    b_far, theirs_2, conv, wq_t, wk, wv_t = lax.optimization_barrier(
        (b_far, theirs_2, conv, wq_t, wk, wv_t)
    )
    conv = pl.pallas_call(
        conv_more_kernel,
        in_specs=[SMEM] + [VMEM] * 8,
        out_specs=VMEM,
        out_shape=near((TOK, C), F32),
        input_output_aliases={8: 0},
        compiler_params=params(20),
        cost_estimate=cost(4),
    )(place, first[1], *mine_2, *theirs_2, conv)
    theirs_3 = send(b_far, SIBLING)
    resid, stats = pl.pallas_call(
        conv_close_kernel,
        in_specs=[SMEM] + [VMEM] * 6,
        out_specs=[VMEM, VMEM],
        out_shape=[near((TOK, C), BF16), shape((16, 2, C), F32)],
        compiler_params=params(20),
    )(place, first[2], b_far, theirs_3, conv, image, kernel_offset_vector[None, :])

    everyone = exchange(stats)
    mine_0, everyone = lax.optimization_barrier((resid, everyone))
    other_0 = send(mine_0, SIBLING)
    c_up = send(mine_0, Z_UP)
    c_down = send(mine_0, Z_DOWN)
    d_own = send(mine_0, X_LO)
    affine = combine(place, everyone, closing_scale_vector, closing_offset_vector)
    c_row = lambda by, at: (x_lo * 8 + (z + by) % 4 * 2 + at) * RP
    d_row = lambda by, at: ((1 - x_lo) * 8 + (z + by) % 4 * 2 + at) * RP
    rows_of = lambda at: [
        [c_row(0, at)],
        [c_row(3, at), c_row(1, at), d_row(0, at)],
        [c_row(2, at), d_row(3, at), d_row(1, at)],
        [d_row(2, at)],
    ]
    mine, theirs = rows_of(core), rows_of(1 - core)

    def rows_place(rows):
        return jnp.stack([first_row, height] + rows)

    acc_shape = (MINE, VROWS, QUERIES)

    top_shape = (MINE, 8, QUERIES)
    pair_scratch = [pltpu.VMEM((QUERIES, 3 * 128), BF16), pltpu.VMEM((HALF_C, QUERIES), BF16)]

    def attend(blocks, rows, state):
        return pl.pallas_call(
            attend_kernel,
            in_specs=[SMEM] + [VMEM] * 8,
            out_specs=[VMEM] * 2,
            out_shape=[near(acc_shape, F32), near(top_shape, F32)],
            scratch_shapes=pair_scratch,
            compiler_params=params(24),
        )(rows_place(rows), affine, query, wk, wv_t, *blocks, *state)

    def held_until(blocks, state):
        return lax.optimization_barrier((blocks, state))

    query, *state = pl.pallas_call(
        open_kernel,
        in_specs=[SMEM] + [VMEM] * 3 + [ANY] + [VMEM] * 2,
        out_specs=[VMEM] * 3,
        out_shape=[
            near((MINE, 2 * HEAD_DIM, QUERIES), BF16),
            near(acc_shape, F32),
            near(top_shape, F32),
        ],
        scratch_shapes=[
            pltpu.VMEM(top_shape, F32),
            pltpu.VMEM((HALF_C, C), BF16),
            pltpu.SemaphoreType.DMA,
        ]
        + pair_scratch,
        compiler_params=params(24),
    )(rows_place(mine[0] + theirs[0]), affine, resid, other_0, wq_t, wk, wv_t)

    mine_1, state = held_until([c_up, c_down, d_own], state)
    c_far = send(mine_1[0], Z_UP)
    d_up = send(mine_1[0], X_LO)
    d_down = send(mine_1[2], Z_DOWN)
    other_1 = [send(mine_1[0], SIBLING)]
    state = attend(mine_1[:2], mine[1][:2], state)
    (late, other_1), state = held_until((mine_1[1:], other_1), state)
    other_1 += [send(block, pairs) for block, pairs in zip(late, SIBLINGS)]
    state = attend([late[1], other_1[0]], mine[1][2:] + theirs[1][:1], state)
    mine_2, state = held_until([c_far, d_up, d_down], state)
    last = send(mine_2[0], X_LO)
    other_2 = [send(block, pairs) for block, pairs in zip(mine_2, SIBLINGS)]
    state = attend(other_1[1:], theirs[1][1:], state)
    state = attend(mine_2[:2], mine[2][:2], state)
    state = attend([mine_2[2], other_2[0]], mine[2][2:] + theirs[2][:1], state)
    (last, other_2), state = held_until((last, other_2), state)
    other_3 = send(last, SIBLING)
    state = attend(other_2[1:], theirs[2][1:], state)
    other_3, state = held_until(other_3, state)

    mixed, others = pl.pallas_call(
        close_kernel,
        in_specs=[SMEM] + [VMEM] * 8,
        out_specs=[VMEM] * 2,
        out_shape=[near((HALF_C, TOK), BF16)] * 2,
        scratch_shapes=[pltpu.VMEM(acc_shape, F32), pltpu.VMEM(top_shape, F32)] + pair_scratch,
        compiler_params=params(24),
    )(rows_place(mine[3] + theirs[3]), affine, query, wk, wv_t, last, other_3, *state)
    other = send(others, SIBLING)
    out = pl.pallas_call(
        finish_kernel,
        in_specs=[SMEM] + [VMEM] * 5,
        out_specs=VMEM,
        out_shape=shape((TOK, C), BF16),
        compiler_params=params(20),
    )(place, mixed, other, resid, out_weight, out_bias[None, :])
    return out.reshape(1, RP, W, C)


def solution(mesh):
    in_specs = (
        P("image", "patch", None, None),
        P("image"),
        P(),
        P(),
        P(None, None, "image", None),
        P(),
        P(),
        P(),
        P(),
        P(),
        P(),
        P(),
        P(),
    )
    out_specs = P("image", "patch", None, None)
    return jax.shard_map(
        per_device, mesh=mesh, in_specs=in_specs, out_specs=out_specs, check_vma=False
    )
```
